32 devices in a mesh: rep: 2 (over y), gx: 4 (over z), gy: 2 (over x), gz: 2 (over core).
Axes of the slice: x: 2, y: 2, z: 4, core: 2. Of those that a mesh axis runs over, the one named last changes fastest.
Arguments:
- seed_state: float32 [9, 16, 32, 256], P(None, ('rep', 'gx'), 'gy', 'gz'), parts along dimension 1, may hold values from -6 to 6
- costate: float32 [9, 16, 32, 256], P(None, ('rep', 'gx'), 'gy', 'gz'), parts along dimension 1, may hold values from -6 to 6
- step_count: int32 [2], P('rep'), parts along dimension 0, may hold values from 4 to 16
Outputs:
- next_state: float32 [9, 16, 32, 256], P(None, ('rep', 'gx'), 'gy', 'gz'), parts along dimension 1
- seed_gradient: float32 [9, 16, 32, 256], P(None, ('rep', 'gx'), 'gy', 'gz'), parts along dimension 1
The draws below stay inside these ranges and needn't reach their ends.
There are 2 independent parts, one for each index of `rep`. The reference program is written for one: setup_inputs(seed, part) draws one part's arguments, and reference() takes and returns one part's arrays. A program takes and returns all parts, laid end to end along the dimension named above; each array names one. Nothing has to cross between parts.
All inputs are finite; a program needn't handle non-finite values.
Results may differ from the reference program's by a relative error of at most 0.00002.
Values sent between devices are 32-bit elements; how exact they have to be, the bound alone decides.
No kernel may reach another device: no remote copies, remote signals or barrier semaphores. Data moves between devices by JAX's collectives and lax.ppermute only.
A program may use at most 128 MiB of HBM per device.

```python
import jax
import jax.numpy as jnp

FIELDS = 9
NX = 8
NY = 32
NZ = 256


def levels(rng, shape, cuts, low, high):
    def one(dim, blocks):
        heights = jax.random.uniform(jax.random.fold_in(jax.random.fold_in(rng, 6), dim), (blocks,), jnp.float32, low / len(cuts), high / len(cuts))
        return jnp.repeat(jnp.exp(heights), shape[dim] // blocks).reshape((-1,) + (1,) * (len(shape) - dim - 1))

    loudness = one(*cuts[0])
    for cut in cuts[1:]:
        loudness = loudness * one(*cut)
    return loudness


def bell_draw(rng, shape, spread, reach, cuts=(), kind=jnp.bfloat16):
    values = spread * jax.random.normal(rng, shape, jnp.float32)
    if cuts:
        values = values * levels(rng, shape, cuts, -0.22, 0.18)
    return jnp.clip(values, -reach, reach).astype(kind)


def setup_inputs(seed: int = 0, part: int = 0) -> dict:
    seeds = jax.random.split(jax.random.key(seed), 4)
    part_keys = jax.random.split(jax.random.fold_in(seeds[3], part), 4)
    seed_state = bell_draw(part_keys[0], (FIELDS, NX, NY, NZ), 1.0, 6.0, ((1, 4), (2, 2), (3, 2)), jnp.float32)
    costate = bell_draw(part_keys[1], (FIELDS, NX, NY, NZ), 1.0, 6.0, ((1, 4), (2, 2), (3, 2)), jnp.float32)
    step_count = jax.random.randint(part_keys[2], (1,), 4, 17).astype(jnp.int32)
    return dict(seed_state=seed_state, costate=costate, step_count=step_count)


VISCOSITY = 0.5
DIFFUSIVITY = 0.2
WEISSENBERG = 2.0
EXTENSIBILITY = 100.0
HORIZON = 1.0
COMPONENT = ((3, 6, 7), (6, 4, 8), (7, 8, 5))
PAIRS = ((0, 0), (1, 1), (2, 2), (0, 1), (0, 2), (1, 2))

def shifted(padded, axis_dim, offset):
    slices = [slice(None), slice(1, -1), slice(1, -1), slice(1, -1)]
    length = padded.shape[axis_dim]
    slices[axis_dim] = slice(1 + offset, length - 1 + offset)
    return padded[tuple(slices)]

def centred(padded, axis_dim):
    return 0.5 * (shifted(padded, axis_dim, 1) - shifted(padded, axis_dim, -1))

def advance(padded, time_step):
    centre = padded[:, 1:-1, 1:-1, 1:-1]
    laplace = -6.0 * centre
    for axis_dim in (1, 2, 3):
        laplace = laplace + shifted(padded, axis_dim, 1) + shifted(padded, axis_dim, -1)
    identity = jnp.array([1.0, 1.0, 1.0, 0.0, 0.0, 0.0], jnp.float32)[:, None, None, None]
    factor = (EXTENSIBILITY - 3.0) / (EXTENSIBILITY - (padded[3] + padded[4] + padded[5]))
    stress = (factor[None] * padded[3:9] - identity) / WEISSENBERG
    stress_slopes = [centred(stress, axis_dim) for axis_dim in (1, 2, 3)]
    grads = [centred(padded[0:3], axis_dim) for axis_dim in (1, 2, 3)]
    outputs = []
    for comp_i in range(3):
        divergence = stress_slopes[0][COMPONENT[comp_i][0] - 3]
        divergence = divergence + stress_slopes[1][COMPONENT[comp_i][1] - 3] + stress_slopes[2][COMPONENT[comp_i][2] - 3]
        outputs.append(centre[comp_i] + time_step * (VISCOSITY * laplace[comp_i] + divergence))
    stress_centre = stress[:, 1:-1, 1:-1, 1:-1]
    for number in range(6):
        comp_i, comp_j = PAIRS[number]
        stretch = jnp.zeros_like(centre[0])
        for axis_k in range(3):
            stretch = stretch + grads[axis_k][comp_i] * centre[COMPONENT[axis_k][comp_j]]
            stretch = stretch + centre[COMPONENT[comp_i][axis_k]] * grads[axis_k][comp_j]
        update = DIFFUSIVITY * laplace[3 + number] + stretch - stress_centre[number]
        outputs.append(centre[3 + number] + time_step * update)
    return jnp.stack(outputs, 0)

def pad_field(fields, width):
    wrapped = jnp.pad(fields, ((0, 0), (width, width), (0, 0), (width, width)), mode='wrap')
    return jnp.pad(wrapped, ((0, 0), (0, 0), (width, width), (0, 0)))

def reference(seed_state, costate, step_count):
    time_step = HORIZON / step_count[0].astype(jnp.float32)

    def forward(fields):
        return advance(pad_field(fields, 1), time_step)
    next_state, pullback = jax.vjp(forward, seed_state)
    raw_gradient, = pullback(costate)
    signs = jnp.array([1.0, -1.0, 1.0, 1.0, 1.0, 1.0, -1.0, 1.0, -1.0], jnp.float32)[:, None, None, None]
    mirrored = jnp.flip(raw_gradient, axis=2) * signs
    return (next_state, 0.5 * (raw_gradient + mirrored))
```

```python
import jax
import jax.numpy as jnp
from jax import lax
from jax.experimental import pallas as pl
from jax.experimental.pallas import tpu as pltpu
from jax.sharding import PartitionSpec as P

VISCOSITY = 0.5
DIFFUSIVITY = 0.2
EXTENSIBILITY = 100.0
HORIZON = 1.0
COMP = ((0, 3, 4), (3, 1, 5), (4, 5, 2))
PAIRS = ((0, 0), (1, 1), (2, 2), (0, 1), (0, 2), (1, 2))
SIGNS = (1.0, -1.0, 1.0, 1.0, 1.0, 1.0, -1.0, 1.0, -1.0)


def swap_even(array, axis):
    size = lax.axis_size(axis)
    return lax.ppermute(array, axis, [(i, i ^ 1) for i in range(size)])


def swap_odd(array, axis):
    size = lax.axis_size(axis)
    pairs = [(i, (i + 1) % size if i % 2 else (i - 1) % size) for i in range(size)]
    return lax.ppermute(array, axis, pairs)


def exchange_x(first, last):
    size = lax.axis_size("gx")
    if size % 2:
        below = lax.ppermute(last, "gx", [(i, (i + 1) % size) for i in range(size)])
        above = lax.ppermute(first, "gx", [((i + 1) % size, i) for i in range(size)])
        return below, above
    even = lax.axis_index("gx") % 2 == 0
    far = swap_odd(jnp.where(even, first, last), "gx")
    near = swap_even(jnp.where(even, last, first), "gx")
    return far, near


def neighbours_y(brick):
    size = lax.axis_size("gy")
    if size == 1:
        return brick
    if size == 2:
        return swap_even(brick, "gy")
    below = lax.ppermute(brick, "gy", [(i, i + 1) for i in range(size - 1)])
    above = lax.ppermute(brick, "gy", [(i + 1, i) for i in range(size - 1)])
    half = brick.shape[2] // 2
    return jnp.concatenate([above[:, :, :half], below[:, :, half:]], axis=2)


def neighbours_z(brick):
    size = lax.axis_size("gz")
    if size == 1:
        return brick
    if size == 2:
        return swap_even(brick, "gz")
    below = lax.ppermute(brick, "gz", [(i, (i + 1) % size) for i in range(size)])
    above = lax.ppermute(brick, "gz", [((i + 1) % size, i) for i in range(size)])
    half = brick.shape[3] // 2
    return jnp.concatenate([above[..., :half], below[..., half:]], axis=3)


class Shifts:
    def __init__(self, rows, lanes):
        self.rows, self.lanes = rows, lanes
        self.row = lax.broadcasted_iota(jnp.int32, (rows, lanes), 0)
        self.lane = lax.broadcasted_iota(jnp.int32, (rows, lanes), 1)
        wall, walls = lax.axis_index("gy"), lax.axis_size("gy")
        self.beyond = ((self.row == 0) & (wall == walls - 1)) | ((self.row == rows - 1) & (wall == 0))

    def clean(self, edge):
        return jnp.where(self.beyond, 0.0, edge)

    def y(self, plane, edge):
        up = pltpu.roll(jnp.where(self.row == 0, edge, plane), self.rows - 1, 0)
        down = pltpu.roll(jnp.where(self.row == self.rows - 1, edge, plane), 1, 0)
        return up, down

    def z(self, plane, edge):
        up = pltpu.roll(jnp.where(self.lane == 0, edge, plane), self.lanes - 1, 1)
        down = pltpu.roll(jnp.where(self.lane == self.lanes - 1, edge, plane), 1, 1)
        return up, down


def stretch_pull(conf, dual, column):
    out = []
    for m in range(3):
        total = 0.0
        for j in range(3):
            term = dual[COMP[m][j]] * conf[COMP[j][column]]
            total = total + (term + term if j == m else term)
        out.append(total)
    return out


def half_factor(conf):
    return (0.5 * (EXTENSIBILITY - 3.0)) / (EXTENSIBILITY - (conf[0] + conf[1] + conf[2]))


def pick_x(far_ref, near_ref, field):
    far, near = far_ref[field], near_ref[field]
    if lax.axis_size("gx") % 2:
        return far, near
    even = jnp.full(far.shape, lax.axis_index("gx") % 2, jnp.int32) == 0
    return jnp.where(even, far, near), jnp.where(even, near, far)


def halo_planes(ref, offset, far_ref, near_ref, count):
    fields = []
    for f in range(count):
        below, above = pick_x(far_ref, near_ref, offset + f)
        fields.append([below] + [ref[f, p] for p in range(ref.shape[1])] + [above])
    return fields


def raw_kernel(steps_ref, seed_ref, dual_ref, far_ref, near_ref, ys_ref, yd_ref, zs_ref, zd_ref, raw_ref):
    _, depth, rows, lanes = seed_ref.shape
    shift = Shifts(rows, lanes)
    time_step = HORIZON / jnp.full((rows, lanes), steps_ref[0], jnp.int32).astype(jnp.float32)
    seed = halo_planes(seed_ref, 0, far_ref, near_ref, 9)
    dual = halo_planes(dual_ref, 9, far_ref, near_ref, 9)
    pull_x = [
        stretch_pull([c[p] for c in seed[3:]], [c[p] for c in dual[3:]], 0) for p in range(depth + 2)
    ]
    for p in range(depth):
        at = p + 1
        conf = [c[at] for c in seed[3:]]
        pulled = [c[at] for c in dual[3:]]
        ey = [shift.clean(yd_ref[f, p]) for f in range(9)]
        ez = [zd_ref[f, p] for f in range(9)]
        eys = [shift.clean(ys_ref[f, p]) for f in range(9)]
        ezs = [zs_ref[f, p] for f in range(9)]
        laps, slopes = [], []
        for f in range(9):
            here = dual[f][at]
            yu, yd = shift.y(here, ey[f])
            zu, zd = shift.z(here, ez[f])
            xu, xd = dual[f][at + 1], dual[f][at - 1]
            laps.append((xu + xd) + (yu + yd) + (zu + zd) - 6.0 * here)
            if f < 3:
                slopes.append((0.5 * (xu - xd), 0.5 * (yu - yd), 0.5 * (zu - zd)))
        grads = []
        for f in range(3):
            here = seed[f][at]
            yu, yd = shift.y(here, eys[f])
            zu, zd = shift.z(here, ezs[f])
            xu, xd = seed[f][at + 1], seed[f][at - 1]
            grads.append((0.5 * (xu - xd), 0.5 * (yu - yd), 0.5 * (zu - zd)))
        pull_y = stretch_pull(conf, pulled, 1)
        pull_z = stretch_pull(conf, pulled, 2)
        edge_y = stretch_pull(eys[3:], ey[3:], 1)
        edge_z = stretch_pull(ezs[3:], ez[3:], 2)
        for m in range(3):
            yu, yd = shift.y(pull_y[m], edge_y[m])
            zu, zd = shift.z(pull_z[m], edge_z[m])
            flux = (pull_x[at + 1][m] - pull_x[at - 1][m]) + (yu - yd) + (zu - zd)
            raw_ref[m, p] = dual[m][at] + time_step * (VISCOSITY * laps[m] - 0.5 * flux)
        half = half_factor(conf)
        stress = []
        for n, (i, j) in enumerate(PAIRS):
            slope = slopes[i][j] if i == j else slopes[i][j] + slopes[j][i]
            stress.append(-(slope + pulled[n]))
        inner = 0.0
        for n in range(6):
            inner = inner + stress[n] * conf[n]
        inner = inner * (half * half) * (2.0 / (EXTENSIBILITY - 3.0))

        def weight(k, j):
            total = 0.0
            for m in range(3):
                term = grads[m][k] * pulled[COMP[m][j]]
                total = total + (term + term if m == j else term)
            return total

        for n, (i, j) in enumerate(PAIRS):
            change = DIFFUSIVITY * laps[3 + n] + half * stress[n]
            change = change + (weight(i, i) + inner if i == j else weight(i, j) + weight(j, i))
            raw_ref[3 + n, p] = pulled[n] + time_step * change


def next_kernel(steps_ref, seed_ref, far_ref, near_ref, ys_ref, zs_ref, next_ref):
    _, depth, rows, lanes = seed_ref.shape
    shift = Shifts(rows, lanes)
    time_step = HORIZON / jnp.full((rows, lanes), steps_ref[0], jnp.int32).astype(jnp.float32)
    seed = halo_planes(seed_ref, 0, far_ref, near_ref, 9)
    halves = [half_factor([c[p] for c in seed[3:]]) for p in range(depth + 2)]
    for p in range(depth):
        at = p + 1
        conf = [c[at] for c in seed[3:]]
        ey = [shift.clean(ys_ref[f, p]) for f in range(9)]
        ez = [zs_ref[f, p] for f in range(9)]
        laps, grads = [], []
        for f in range(9):
            here = seed[f][at]
            yu, yd = shift.y(here, ey[f])
            zu, zd = shift.z(here, ez[f])
            xu, xd = seed[f][at + 1], seed[f][at - 1]
            laps.append((xu + xd) + (yu + yd) + (zu + zd) - 6.0 * here)
            if f < 3:
                grads.append((0.5 * (xu - xd), 0.5 * (yu - yd), 0.5 * (zu - zd)))
        half = halves[at]
        half_y, half_z = half_factor(ey[3:]), half_factor(ez[3:])
        for i in range(3):
            cx, cy, cz = COMP[i]
            yu, yd = shift.y(half * conf[cy], half_y * ey[3 + cy])
            zu, zd = shift.z(half * conf[cz], half_z * ez[3 + cz])
            xu = halves[at + 1] * seed[3 + cx][at + 1]
            xd = halves[at - 1] * seed[3 + cx][at - 1]
            divergence = 0.5 * ((xu - xd) + (yu - yd) + (zu - zd))
            next_ref[i, p] = seed[i][at] + time_step * (VISCOSITY * laps[i] + divergence)
        for n, (i, j) in enumerate(PAIRS):
            stretch = 0.0
            for k in range(3):
                term = grads[i][k] * conf[COMP[k][j]]
                stretch = stretch + (term + term if i == j else term + grads[j][k] * conf[COMP[k][i]])
            stress = half * conf[n] - (0.5 if i == j else 0.0)
            next_ref[3 + n, p] = conf[n] + time_step * (DIFFUSIVITY * laps[3 + n] + stretch - stress)


def call(kernel, shape, steps, *arrays):
    vmem = pl.BlockSpec(memory_space=pltpu.VMEM)
    return pl.pallas_call(
        kernel,
        out_shape=jax.ShapeDtypeStruct(shape, jnp.float32),
        in_specs=[pl.BlockSpec(memory_space=pltpu.SMEM)] + [vmem] * len(arrays),
        out_specs=vmem,
        cost_estimate=pl.CostEstimate(flops=4_000_000, bytes_accessed=1_000_000, transcendentals=0),
        compiler_params=pltpu.CompilerParams(vmem_limit_bytes=16 * 1024 * 1024),
    )(steps, *arrays)


def per_device(seed_state, costate, step_count):
    first = jnp.concatenate([seed_state[:, 0], costate[:, 0]], 0)
    last = jnp.concatenate([seed_state[:, -1], costate[:, -1]], 0)
    far, near = exchange_x(first, last)
    ys, yd = neighbours_y(seed_state), neighbours_y(costate)
    zs, zd = neighbours_z(seed_state), neighbours_z(costate)
    raw = call(raw_kernel, seed_state.shape, step_count, seed_state, costate, far, near, ys, yd, zs, zd)
    walls = lax.axis_size("gy")
    partner = lax.ppermute(raw, "gy", [(i, walls - 1 - i) for i in range(walls)])
    next_state = call(next_kernel, seed_state.shape, step_count, seed_state, far, near, ys, zs)
    signs = jnp.array(SIGNS, jnp.float32)[:, None, None, None]
    seed_gradient = 0.5 * (raw + jnp.flip(partner, axis=2) * signs)
    return next_state, seed_gradient


def solution(mesh):
    placed = P(None, ("rep", "gx"), "gy", "gz")
    return jax.shard_map(
        per_device,
        mesh=mesh,
        in_specs=(placed, placed, P("rep")),
        out_specs=(placed, placed),
        check_vma=False,
    )
```

```python
import functools

import jax
import jax.numpy as jnp
from jax import lax
from jax.experimental import pallas as pl
from jax.experimental.pallas import tpu as pltpu
from jax.sharding import PartitionSpec as P

VISCOSITY = 0.5
DIFFUSIVITY = 0.2
EXTENSIBILITY = 100.0
HORIZON = 1.0
COMP = ((0, 3, 4), (3, 1, 5), (4, 5, 2))
PAIRS = ((0, 0), (1, 1), (2, 2), (0, 1), (0, 2), (1, 2))
SIGNS = (1.0, -1.0, 1.0, 1.0, 1.0, 1.0, -1.0, 1.0, -1.0)


def ring(array, axis, step):
    size = lax.axis_size(axis)
    return lax.ppermute(array, axis, [(i, (i + step) % size) for i in range(size)])


def line(array, axis, step):
    size = lax.axis_size(axis)
    return lax.ppermute(array, axis, [(i, i + step) for i in range(size) if 0 <= i + step < size])


def rows_y(bricks):
    size = lax.axis_size("gy")
    fields, planes, _, lanes = bricks.shape
    first = bricks[:, :, 0].reshape(fields * planes, lanes)
    last = bricks[:, :, -1].reshape(fields * planes, lanes)
    if size == 1:
        return first, last
    if size == 2:
        other = ring(jnp.where(lax.axis_index("gy") == 0, last, first), "gy", 1)
        return other, other
    return line(first, "gy", -1), line(last, "gy", 1)


def neighbours_z(bricks):
    size = lax.axis_size("gz")
    if size == 1:
        return bricks
    if size == 2:
        return ring(bricks, "gz", 1)
    half = bricks.shape[3] // 2
    return jnp.concatenate([ring(bricks, "gz", -1)[..., :half], ring(bricks, "gz", 1)[..., half:]], axis=3)


class Shifts:
    def __init__(self, rows, lanes):
        self.rows, self.lanes = rows, lanes
        self.row = lax.broadcasted_iota(jnp.int32, (rows, lanes), 0)
        self.lane = lax.broadcasted_iota(jnp.int32, (rows, lanes), 1)
        wall, walls = lax.axis_index("gy"), lax.axis_size("gy")
        self.last_wall = jnp.full((rows, lanes), wall, jnp.int32) == walls - 1
        self.first_wall = jnp.full((rows, lanes), wall, jnp.int32) == 0

    def edges(self, above_ref, below_ref, place):
        shape = (self.rows, self.lanes)
        above = jnp.broadcast_to(above_ref[pl.ds(place, 1), :], shape)
        below = jnp.broadcast_to(below_ref[pl.ds(place, 1), :], shape)
        return jnp.where(self.last_wall, 0.0, above), jnp.where(self.first_wall, 0.0, below)

    def y(self, plane, above, below):
        up = jnp.where(self.row == self.rows - 1, above, pltpu.roll(plane, self.rows - 1, 0))
        down = jnp.where(self.row == 0, below, pltpu.roll(plane, 1, 0))
        return up, down

    def z(self, plane, edge):
        up = pltpu.roll(jnp.where(self.lane == 0, edge, plane), self.lanes - 1, 1)
        down = pltpu.roll(jnp.where(self.lane == self.lanes - 1, edge, plane), 1, 1)
        return up, down


def stretch_pull(conf, dual, column):
    out = []
    for m in range(3):
        total = 0.0
        for j in range(3):
            term = dual[COMP[m][j]] * conf[COMP[j][column]]
            total = total + (term + term if j == m else term)
        out.append(total)
    return out


def half_factor(conf):
    return (0.5 * (EXTENSIBILITY - 3.0)) / (EXTENSIBILITY - (conf[0] + conf[1] + conf[2]))


def halo_planes(ref, start, count, offset, below_ref, above_ref):
    depth = ref.shape[1]
    fields = []
    for f in range(ref.shape[0]):
        planes = []
        for p in range(start - 1, start + count + 1):
            if p < 0:
                planes.append(below_ref[offset + f])
            elif p == depth:
                planes.append(above_ref[offset + f])
            else:
                planes.append(ref[f, p])
        fields.append(planes)
    return fields


def raw_kernel(start, count, has_below, has_above, *refs):
    steps_ref, seed_ref, dual_ref, ya_ref, yb_ref, z_ref, *halo_refs, raw_ref = refs
    below_ref = halo_refs[0] if has_below else None
    above_ref = halo_refs[-1] if has_above else None
    _, depth, rows, lanes = seed_ref.shape
    shift = Shifts(rows, lanes)
    time_step = HORIZON / jnp.full((rows, lanes), steps_ref[0], jnp.int32).astype(jnp.float32)
    seed = halo_planes(seed_ref, start, count, 0, below_ref, above_ref)
    dual = halo_planes(dual_ref, start, count, 9, below_ref, above_ref)
    pull_x = [
        stretch_pull([c[p] for c in seed[3:]], [c[p] for c in dual[3:]], 0) for p in range(count + 2)
    ]
    for q in range(count):
        p, at = start + q, q + 1
        conf = [c[at] for c in seed[3:]]
        pulled = [c[at] for c in dual[3:]]
        seed_y = [shift.edges(ya_ref, yb_ref, f * depth + p) for f in range(9)]
        dual_y = [shift.edges(ya_ref, yb_ref, (9 + f) * depth + p) for f in range(9)]
        seed_z = [z_ref[f, p] for f in range(9)]
        dual_z = [z_ref[9 + f, p] for f in range(9)]
        laps, slopes = [], []
        for f in range(9):
            here = dual[f][at]
            yu, yd = shift.y(here, *dual_y[f])
            zu, zd = shift.z(here, dual_z[f])
            xu, xd = dual[f][at + 1], dual[f][at - 1]
            laps.append((xu + xd) + (yu + yd) + (zu + zd) - 6.0 * here)
            if f < 3:
                slopes.append((0.5 * (xu - xd), 0.5 * (yu - yd), 0.5 * (zu - zd)))
        grads = []
        for f in range(3):
            here = seed[f][at]
            yu, yd = shift.y(here, *seed_y[f])
            zu, zd = shift.z(here, seed_z[f])
            xu, xd = seed[f][at + 1], seed[f][at - 1]
            grads.append((0.5 * (xu - xd), 0.5 * (yu - yd), 0.5 * (zu - zd)))
        pull_y = stretch_pull(conf, pulled, 1)
        pull_z = stretch_pull(conf, pulled, 2)
        above_y = stretch_pull([c[0] for c in seed_y[3:]], [c[0] for c in dual_y[3:]], 1)
        below_y = stretch_pull([c[1] for c in seed_y[3:]], [c[1] for c in dual_y[3:]], 1)
        edge_z = stretch_pull(seed_z[3:], dual_z[3:], 2)
        for m in range(3):
            yu, yd = shift.y(pull_y[m], above_y[m], below_y[m])
            zu, zd = shift.z(pull_z[m], edge_z[m])
            flux = (pull_x[at + 1][m] - pull_x[at - 1][m]) + (yu - yd) + (zu - zd)
            raw_ref[m, q] = dual[m][at] + time_step * (VISCOSITY * laps[m] - 0.5 * flux)
        half = half_factor(conf)
        stress = []
        for n, (i, j) in enumerate(PAIRS):
            slope = slopes[i][j] if i == j else slopes[i][j] + slopes[j][i]
            stress.append(-(slope + pulled[n]))
        inner = 0.0
        for n in range(6):
            inner = inner + stress[n] * conf[n]
        inner = inner * (half * half) * (2.0 / (EXTENSIBILITY - 3.0))

        def weight(k, j):
            total = 0.0
            for m in range(3):
                term = grads[m][k] * pulled[COMP[m][j]]
                total = total + (term + term if m == j else term)
            return total

        for n, (i, j) in enumerate(PAIRS):
            change = DIFFUSIVITY * laps[3 + n] + half * stress[n]
            change = change + (weight(i, i) + inner if i == j else weight(i, j) + weight(j, i))
            raw_ref[3 + n, q] = pulled[n] + time_step * change


def next_kernel(steps_ref, seed_ref, ya_ref, yb_ref, z_ref, below_ref, above_ref, next_ref):
    _, depth, rows, lanes = seed_ref.shape
    shift = Shifts(rows, lanes)
    time_step = HORIZON / jnp.full((rows, lanes), steps_ref[0], jnp.int32).astype(jnp.float32)
    seed = halo_planes(seed_ref, 0, depth, 0, below_ref, above_ref)
    halves = [half_factor([c[p] for c in seed[3:]]) for p in range(depth + 2)]
    for p in range(depth):
        at = p + 1
        conf = [c[at] for c in seed[3:]]
        ey = [shift.edges(ya_ref, yb_ref, f * depth + p) for f in range(9)]
        ez = [z_ref[f, p] for f in range(9)]
        laps, grads = [], []
        for f in range(9):
            here = seed[f][at]
            yu, yd = shift.y(here, *ey[f])
            zu, zd = shift.z(here, ez[f])
            xu, xd = seed[f][at + 1], seed[f][at - 1]
            laps.append((xu + xd) + (yu + yd) + (zu + zd) - 6.0 * here)
            if f < 3:
                grads.append((0.5 * (xu - xd), 0.5 * (yu - yd), 0.5 * (zu - zd)))
        half = halves[at]
        half_above, half_below = half_factor([c[0] for c in ey[3:]]), half_factor([c[1] for c in ey[3:]])
        half_z = half_factor(ez[3:])
        for i in range(3):
            cx, cy, cz = COMP[i]
            yu, yd = shift.y(half * conf[cy], half_above * ey[3 + cy][0], half_below * ey[3 + cy][1])
            zu, zd = shift.z(half * conf[cz], half_z * ez[3 + cz])
            xu = halves[at + 1] * seed[3 + cx][at + 1]
            xd = halves[at - 1] * seed[3 + cx][at - 1]
            divergence = 0.5 * ((xu - xd) + (yu - yd) + (zu - zd))
            next_ref[i, p] = seed[i][at] + time_step * (VISCOSITY * laps[i] + divergence)
        for n, (i, j) in enumerate(PAIRS):
            stretch = 0.0
            for k in range(3):
                term = grads[i][k] * conf[COMP[k][j]]
                stretch = stretch + (term + term if i == j else term + grads[j][k] * conf[COMP[k][i]])
            stress = half * conf[n] - (0.5 if i == j else 0.0)
            next_ref[3 + n, p] = conf[n] + time_step * (DIFFUSIVITY * laps[3 + n] + stretch - stress)


def call(kernel, shape, steps, *arrays):
    vmem = pl.BlockSpec(memory_space=pltpu.VMEM)
    return pl.pallas_call(
        kernel,
        out_shape=jax.ShapeDtypeStruct(shape, jnp.float32),
        in_specs=[pl.BlockSpec(memory_space=pltpu.SMEM)] + [vmem] * len(arrays),
        out_specs=vmem,
        cost_estimate=pl.CostEstimate(flops=4_000_000, bytes_accessed=1_000_000, transcendentals=0),
        compiler_params=pltpu.CompilerParams(vmem_limit_bytes=16 * 1024 * 1024),
    )(steps, *arrays)


def per_device(seed_state, costate, step_count):
    depth = seed_state.shape[1]
    first = jnp.concatenate([seed_state[:, 0], costate[:, 0]], 0)
    last = jnp.concatenate([seed_state[:, -1], costate[:, -1]], 0)
    below = ring(last, "gx", 1)
    above = ring(first, "gx", -1)
    both = jnp.concatenate([seed_state, costate], 0)
    ya, yb = rows_y(both)
    z = neighbours_z(both)
    walls = lax.axis_size("gy")
    signs = jnp.array(SIGNS, jnp.float32)[:, None, None, None]
    parts = []
    for start, count in ((0, depth - 1), (depth - 1, 1)):
        if count == 0:
            continue
        has_below, has_above = start == 0, start + count == depth
        raw = call(
            functools.partial(raw_kernel, start, count, has_below, has_above),
            (9, count) + seed_state.shape[2:],
            step_count,
            *(seed_state, costate, ya, yb, z),
            *((below,) if has_below else ()),
            *((above,) if has_above else ()),
        )
        partner = lax.ppermute(raw, "gy", [(i, walls - 1 - i) for i in range(walls)])
        parts.append(0.5 * (raw + jnp.flip(partner, axis=2) * signs))
    next_state = call(next_kernel, seed_state.shape, step_count, seed_state, ya, yb, z, below, above)
    return next_state, jnp.concatenate(parts, axis=1)


def solution(mesh):
    placed = P(None, ("rep", "gx"), "gy", "gz")
    return jax.shard_map(
        per_device,
        mesh=mesh,
        in_specs=(placed, placed, P("rep")),
        out_specs=(placed, placed),
        check_vma=False,
    )
```

```python
import functools

import jax
import jax.numpy as jnp
from jax import lax
from jax.experimental import pallas as pl
from jax.experimental.pallas import tpu as pltpu
from jax.sharding import PartitionSpec as P

VISCOSITY = 0.5
DIFFUSIVITY = 0.2
EXTENSIBILITY = 100.0
HORIZON = 1.0
COMP = ((0, 3, 4), (3, 1, 5), (4, 5, 2))
PAIRS = ((0, 0), (1, 1), (2, 2), (0, 1), (0, 2), (1, 2))
SIGNS = (1.0, -1.0, 1.0, 1.0, 1.0, 1.0, -1.0, 1.0, -1.0)


def facing():
    return lax.axis_index("gz") % 2


def place_of(step, depth):
    return jnp.where(facing() == 0, step, depth - 1 - step)


def ahead(array, step):
    size, cores = lax.axis_size("gx"), lax.axis_size("gz")
    pairs = []
    for i in range(size):
        for core in range(cores):
            way = step if core % 2 == 0 else -step
            pairs.append((i * cores + core, (i + way) % size * cores + core))
    return lax.ppermute(array, ("gx", "gz"), pairs)


def ring(array, axis, step):
    size = lax.axis_size(axis)
    return lax.ppermute(array, axis, [(i, (i + step) % size) for i in range(size)])


def line(array, axis, step):
    size = lax.axis_size(axis)
    return lax.ppermute(array, axis, [(i, i + step) for i in range(size) if 0 <= i + step < size])


def pack_kernel(seed_ref, dual_ref, lanes_ref, *rows_refs):
    fields, depth, rows, lanes = seed_ref.shape
    half = lanes // 2
    if len(rows_refs) == 1:
        places = [jnp.where(lax.axis_index("gy") == 0, rows - 1, 0)]
    else:
        places = [0, rows - 1]
    lane = lax.broadcasted_iota(jnp.int32, (rows, lanes), 1)
    packed = [jnp.zeros((rows, lanes), jnp.float32)] * lanes_ref.shape[0]
    for f in range(2 * fields):
        ref = seed_ref if f < fields else dual_ref
        for p in range(depth):
            n = f * depth + p
            for place, rows_ref in zip(places, rows_refs):
                rows_ref[pl.ds(n, 1), :] = ref[f % fields, p, pl.ds(place, 1), :]
            group, slot = divmod(n, half)
            plane = ref[f % fields, p]
            first = turned(plane, slot)
            last = turned(plane, half + slot + 1 - lanes)
            packed[group] = jnp.where(lane == slot, first, jnp.where(lane == half + slot, last, packed[group]))
    for group, plane in enumerate(packed):
        lanes_ref[group] = plane


def unpack_kernel(above_ref, below_ref, edges_ref):
    fields, depth, rows, lanes = edges_ref.shape
    half = lanes // 2
    lane = lax.broadcasted_iota(jnp.int32, (rows, lanes), 1)
    for f in range(fields):
        for p in range(depth):
            group, slot = divmod(f * depth + p, half)
            above = turned(above_ref[group], -slot)
            below = turned(below_ref[group], lanes - 1 - half - slot)
            edges_ref[f, p] = jnp.where(lane < half, above, below)


def turned(plane, step):
    step = step % plane.shape[1]
    return pltpu.roll(plane, step, 1) if step else plane


def estimate(bytes_accessed):
    return pl.CostEstimate(flops=1_000_000, bytes_accessed=bytes_accessed, transcendentals=0)


def grant():
    return pltpu.CompilerParams(vmem_limit_bytes=16 * 1024 * 1024)


def pack(seed_state, costate):
    fields, depth, rows, lanes = seed_state.shape
    count = 2 * fields * depth
    groups = -(-count // (lanes // 2))
    vmem = pl.BlockSpec(memory_space=pltpu.VMEM)
    shapes = [jax.ShapeDtypeStruct((groups, rows, lanes), jnp.float32)]
    shapes += [jax.ShapeDtypeStruct((count, lanes), jnp.float32)] * (1 if lax.axis_size("gy") == 2 else 2)
    return pl.pallas_call(
        pack_kernel,
        out_shape=shapes,
        in_specs=[vmem] * 2,
        out_specs=[vmem] * len(shapes),
        cost_estimate=estimate(300_000),
        compiler_params=grant(),
    )(seed_state, costate)


def rows_y(packed):
    if len(packed) == 1:
        other = ring(packed[0], "gy", 1)
        return other, other
    first, last = packed
    if lax.axis_size("gy") == 1:
        return first, last
    return line(first, "gy", -1), line(last, "gy", 1)


def lanes_z(packed):
    size = lax.axis_size("gz")
    if size == 1:
        return packed, packed
    if size == 2:
        other = ring(packed, "gz", 1)
        return other, other
    return ring(packed, "gz", -1), ring(packed, "gz", 1)


class Shifts:
    def __init__(self, rows, lanes):
        self.rows, self.lanes = rows, lanes
        self.row = lax.broadcasted_iota(jnp.int32, (rows, lanes), 0)
        self.lane = lax.broadcasted_iota(jnp.int32, (rows, lanes), 1)
        wall, walls = lax.axis_index("gy"), lax.axis_size("gy")
        self.last_wall = jnp.full((rows, lanes), wall, jnp.int32) == walls - 1
        self.first_wall = jnp.full((rows, lanes), wall, jnp.int32) == 0

    def edges(self, above_ref, below_ref, place):
        shape = (self.rows, self.lanes)
        above = jnp.broadcast_to(above_ref[pl.ds(place, 1), :], shape)
        below = jnp.broadcast_to(below_ref[pl.ds(place, 1), :], shape)
        return jnp.where(self.last_wall, 0.0, above), jnp.where(self.first_wall, 0.0, below)

    def y(self, plane, above, below):
        up = jnp.where(self.row == self.rows - 1, above, pltpu.roll(plane, self.rows - 1, 0))
        down = jnp.where(self.row == 0, below, pltpu.roll(plane, 1, 0))
        return up, down

    def z(self, plane, edge):
        up = pltpu.roll(jnp.where(self.lane == 0, edge, plane), self.lanes - 1, 1)
        down = pltpu.roll(jnp.where(self.lane == self.lanes - 1, edge, plane), 1, 1)
        return up, down


def stretch_pull(conf, dual, column):
    out = []
    for m in range(3):
        total = 0.0
        for j in range(3):
            term = dual[COMP[m][j]] * conf[COMP[j][column]]
            total = total + (term + term if j == m else term)
        out.append(total)
    return out


def half_factor(conf):
    return (0.5 * (EXTENSIBILITY - 3.0)) / (EXTENSIBILITY - (conf[0] + conf[1] + conf[2]))


def halo_planes(ref, start, count, offset, behind_ref, ahead_ref):
    depth = ref.shape[1]
    fields = []
    for f in range(9):
        planes = []
        for q in range(start - 1, start + count + 1):
            if q < 0:
                planes.append(behind_ref[offset + f])
            elif q == depth:
                planes.append(ahead_ref[offset + f])
            else:
                planes.append(ref[f, place_of(q, depth)])
        fields.append(planes)
    return fields


def half_way(shape):
    return jnp.where(jnp.full(shape, facing(), jnp.int32) == 0, 0.5, -0.5)


def raw_kernel(start, count, has_behind, has_ahead, *refs):
    steps_ref, seed_ref, dual_ref, ya_ref, yb_ref, z_ref, *halo_refs, raw_ref = refs
    behind_ref = halo_refs[0] if has_behind else None
    ahead_ref = halo_refs[-1] if has_ahead else None
    _, depth, rows, lanes = seed_ref.shape
    shift = Shifts(rows, lanes)
    way = half_way((rows, lanes))
    time_step = HORIZON / jnp.full((rows, lanes), steps_ref[0], jnp.int32).astype(jnp.float32)
    seed = halo_planes(seed_ref, start, count, 0, behind_ref, ahead_ref)
    dual = halo_planes(dual_ref, start, count, 9, behind_ref, ahead_ref)
    pull_x = [
        stretch_pull([c[p] for c in seed[3:]], [c[p] for c in dual[3:]], 0) for p in range(count + 2)
    ]
    for q in range(count):
        p, at = place_of(start + q, depth), q + 1
        conf = [c[at] for c in seed[3:]]
        pulled = [c[at] for c in dual[3:]]
        seed_y = [shift.edges(ya_ref, yb_ref, f * depth + p) for f in range(9)]
        dual_y = [shift.edges(ya_ref, yb_ref, (9 + f) * depth + p) for f in range(9)]
        seed_z = [z_ref[f, p] for f in range(9)]
        dual_z = [z_ref[9 + f, p] for f in range(9)]
        laps, slopes = [], []
        for f in range(9):
            here = dual[f][at]
            yu, yd = shift.y(here, *dual_y[f])
            zu, zd = shift.z(here, dual_z[f])
            xu, xd = dual[f][at + 1], dual[f][at - 1]
            laps.append((xu + xd) + (yu + yd) + (zu + zd) - 6.0 * here)
            if f < 3:
                slopes.append((way * (xu - xd), 0.5 * (yu - yd), 0.5 * (zu - zd)))
        grads = []
        for f in range(3):
            here = seed[f][at]
            yu, yd = shift.y(here, *seed_y[f])
            zu, zd = shift.z(here, seed_z[f])
            xu, xd = seed[f][at + 1], seed[f][at - 1]
            grads.append((way * (xu - xd), 0.5 * (yu - yd), 0.5 * (zu - zd)))
        pull_y = stretch_pull(conf, pulled, 1)
        pull_z = stretch_pull(conf, pulled, 2)
        above_y = stretch_pull([c[0] for c in seed_y[3:]], [c[0] for c in dual_y[3:]], 1)
        below_y = stretch_pull([c[1] for c in seed_y[3:]], [c[1] for c in dual_y[3:]], 1)
        edge_z = stretch_pull(seed_z[3:], dual_z[3:], 2)
        for m in range(3):
            yu, yd = shift.y(pull_y[m], above_y[m], below_y[m])
            zu, zd = shift.z(pull_z[m], edge_z[m])
            flux = way * (pull_x[at + 1][m] - pull_x[at - 1][m]) + 0.5 * ((yu - yd) + (zu - zd))
            raw_ref[m, q] = dual[m][at] + time_step * (VISCOSITY * laps[m] - flux)
        half = half_factor(conf)
        stress = []
        for n, (i, j) in enumerate(PAIRS):
            slope = slopes[i][j] if i == j else slopes[i][j] + slopes[j][i]
            stress.append(-(slope + pulled[n]))
        inner = 0.0
        for n in range(6):
            inner = inner + stress[n] * conf[n]
        inner = inner * (half * half) * (2.0 / (EXTENSIBILITY - 3.0))

        def weight(k, j):
            total = 0.0
            for m in range(3):
                term = grads[m][k] * pulled[COMP[m][j]]
                total = total + (term + term if m == j else term)
            return total

        for n, (i, j) in enumerate(PAIRS):
            change = DIFFUSIVITY * laps[3 + n] + half * stress[n]
            change = change + (weight(i, i) + inner if i == j else weight(i, j) + weight(j, i))
            raw_ref[3 + n, q] = pulled[n] + time_step * change


def next_kernel(steps_ref, seed_ref, ya_ref, yb_ref, z_ref, behind_ref, ahead_ref, next_ref):
    _, depth, rows, lanes = seed_ref.shape
    shift = Shifts(rows, lanes)
    way = half_way((rows, lanes))
    time_step = HORIZON / jnp.full((rows, lanes), steps_ref[0], jnp.int32).astype(jnp.float32)
    seed = halo_planes(seed_ref, 0, depth, 0, behind_ref, ahead_ref)
    halves = [half_factor([c[p] for c in seed[3:]]) for p in range(depth + 2)]
    for q in range(depth):
        p, at = place_of(q, depth), q + 1
        conf = [c[at] for c in seed[3:]]
        ey = [shift.edges(ya_ref, yb_ref, f * depth + p) for f in range(9)]
        ez = [z_ref[f, p] for f in range(9)]
        laps, grads = [], []
        for f in range(9):
            here = seed[f][at]
            yu, yd = shift.y(here, *ey[f])
            zu, zd = shift.z(here, ez[f])
            xu, xd = seed[f][at + 1], seed[f][at - 1]
            laps.append((xu + xd) + (yu + yd) + (zu + zd) - 6.0 * here)
            if f < 3:
                grads.append((way * (xu - xd), 0.5 * (yu - yd), 0.5 * (zu - zd)))
        half = halves[at]
        half_above, half_below = half_factor([c[0] for c in ey[3:]]), half_factor([c[1] for c in ey[3:]])
        half_z = half_factor(ez[3:])
        for i in range(3):
            cx, cy, cz = COMP[i]
            yu, yd = shift.y(half * conf[cy], half_above * ey[3 + cy][0], half_below * ey[3 + cy][1])
            zu, zd = shift.z(half * conf[cz], half_z * ez[3 + cz])
            xu = halves[at + 1] * seed[3 + cx][at + 1]
            xd = halves[at - 1] * seed[3 + cx][at - 1]
            divergence = way * (xu - xd) + 0.5 * ((yu - yd) + (zu - zd))
            next_ref[i, p] = seed[i][at] + time_step * (VISCOSITY * laps[i] + divergence)
        for n, (i, j) in enumerate(PAIRS):
            stretch = 0.0
            for k in range(3):
                term = grads[i][k] * conf[COMP[k][j]]
                stretch = stretch + (term + term if i == j else term + grads[j][k] * conf[COMP[k][i]])
            stress = half * conf[n] - (0.5 if i == j else 0.0)
            next_ref[3 + n, p] = conf[n] + time_step * (DIFFUSIVITY * laps[3 + n] + stretch - stress)


def average_kernel(*refs):
    *pairs, out_ref = refs
    step = 0
    for raw_ref, image_ref in zip(pairs[::2], pairs[1::2]):
        for q in range(raw_ref.shape[1]):
            place = place_of(step, out_ref.shape[1])
            for f, sign in enumerate(SIGNS):
                raw, image = raw_ref[f, q], image_ref[f, q]
                out_ref[f, place] = 0.5 * (raw + image if sign > 0 else raw - image)
            step += 1


def call(kernel, shape, steps, *arrays):
    vmem = pl.BlockSpec(memory_space=pltpu.VMEM)
    scalars = [pl.BlockSpec(memory_space=pltpu.SMEM)] * len(steps)
    return pl.pallas_call(
        kernel,
        out_shape=jax.ShapeDtypeStruct(shape, jnp.float32),
        in_specs=scalars + [vmem] * len(arrays),
        out_specs=vmem,
        cost_estimate=estimate(1_000_000),
        compiler_params=grant(),
    )(*steps, *arrays)


def per_device(seed_state, costate, step_count):
    depth = seed_state.shape[1]
    start_face, end_face = (jnp.concatenate([x[:, p] for x in (seed_state, costate)], 0) for p in (0, -1))
    upwards = facing() == 0
    last = jnp.where(upwards, end_face, start_face)
    first = jnp.where(upwards, start_face, end_face)
    behind = ahead(last, 1)
    front = ahead(first, -1)
    lanes, *rows = pack(seed_state, costate)
    ya, yb = rows_y(rows)
    z = call(unpack_kernel, (18,) + seed_state.shape[1:], (), *lanes_z(lanes))
    walls = lax.axis_size("gy")
    pairs = []
    for start, count in ((0, depth - 1), (depth - 1, 1)):
        if count == 0:
            continue
        has_behind, has_ahead = start == 0, start + count == depth
        raw = call(
            functools.partial(raw_kernel, start, count, has_behind, has_ahead),
            (9, count) + seed_state.shape[2:],
            (step_count,),
            *(seed_state, costate, ya, yb, z),
            *((behind,) if has_behind else ()),
            *((front,) if has_ahead else ()),
        )
        partner = lax.ppermute(raw, "gy", [(i, walls - 1 - i) for i in range(walls)])
        pairs += [raw, jnp.flip(partner, axis=2)]
    next_state = call(next_kernel, seed_state.shape, (step_count,), seed_state, ya, yb, z, behind, front)
    return next_state, call(average_kernel, seed_state.shape, (), *pairs)


def solution(mesh):
    placed = P(None, ("rep", "gx"), "gy", "gz")
    return jax.shard_map(
        per_device,
        mesh=mesh,
        in_specs=(placed, placed, P("rep")),
        out_specs=(placed, placed),
        check_vma=False,
    )
```

```python
import functools

import jax
import jax.numpy as jnp
from jax import lax
from jax.experimental import pallas as pl
from jax.experimental.pallas import tpu as pltpu
from jax.sharding import PartitionSpec as P

VISCOSITY = 0.5
DIFFUSIVITY = 0.2
EXTENSIBILITY = 100.0
HORIZON = 1.0
COMP = ((0, 3, 4), (3, 1, 5), (4, 5, 2))
PAIRS = ((0, 0), (1, 1), (2, 2), (0, 1), (0, 2), (1, 2))
SIGNS = (1.0, -1.0, 1.0, 1.0, 1.0, 1.0, -1.0, 1.0, -1.0)


def ring(array, axis, step):
    size = lax.axis_size(axis)
    return lax.ppermute(array, axis, [(i, (i + step) % size) for i in range(size)])


def line(array, axis, step):
    size = lax.axis_size(axis)
    return lax.ppermute(array, axis, [(i, i + step) for i in range(size) if 0 <= i + step < size])


def pack_kernel(seed_ref, dual_ref, lanes_ref, *rows_refs):
    fields, depth, rows, lanes = seed_ref.shape
    half = lanes // 2
    if len(rows_refs) == 1:
        places = [jnp.where(lax.axis_index("gy") == 0, rows - 1, 0)]
    else:
        places = [0, rows - 1]
    lane = lax.broadcasted_iota(jnp.int32, (rows, lanes), 1)
    packed = [jnp.zeros((rows, lanes), jnp.float32)] * lanes_ref.shape[0]
    for f in range(2 * fields):
        ref = seed_ref if f < fields else dual_ref
        for p in range(depth):
            n = f * depth + p
            for place, rows_ref in zip(places, rows_refs):
                rows_ref[pl.ds(n, 1), :] = ref[f % fields, p, pl.ds(place, 1), :]
            group, slot = divmod(n, half)
            plane = ref[f % fields, p]
            first = turned(plane, slot)
            last = turned(plane, half + slot + 1 - lanes)
            packed[group] = jnp.where(lane == slot, first, jnp.where(lane == half + slot, last, packed[group]))
    for group, plane in enumerate(packed):
        lanes_ref[group] = plane


def unpack_kernel(above_ref, below_ref, edges_ref):
    fields, depth, rows, lanes = edges_ref.shape
    half = lanes // 2
    lane = lax.broadcasted_iota(jnp.int32, (rows, lanes), 1)
    for f in range(fields):
        for p in range(depth):
            group, slot = divmod(f * depth + p, half)
            above = turned(above_ref[group], -slot)
            below = turned(below_ref[group], lanes - 1 - half - slot)
            edges_ref[f, p] = jnp.where(lane < half, above, below)


def turned(plane, step):
    step = step % plane.shape[1]
    return pltpu.roll(plane, step, 1) if step else plane


def estimate(bytes_accessed):
    return pl.CostEstimate(flops=1_000_000, bytes_accessed=bytes_accessed, transcendentals=0)


def grant():
    return pltpu.CompilerParams(vmem_limit_bytes=16 * 1024 * 1024)


def pack(seed_state, costate):
    fields, depth, rows, lanes = seed_state.shape
    count = 2 * fields * depth
    groups = -(-count // (lanes // 2))
    vmem = pl.BlockSpec(memory_space=pltpu.VMEM)
    shapes = [jax.ShapeDtypeStruct((groups, rows, lanes), jnp.float32)]
    shapes += [jax.ShapeDtypeStruct((count, lanes), jnp.float32)] * (1 if lax.axis_size("gy") == 2 else 2)
    return pl.pallas_call(
        pack_kernel,
        out_shape=shapes,
        in_specs=[vmem] * 2,
        out_specs=[vmem] * len(shapes),
        cost_estimate=estimate(300_000),
        compiler_params=grant(),
    )(seed_state, costate)


def rows_y(packed):
    if len(packed) == 1:
        other = ring(packed[0], "gy", 1)
        return other, other
    first, last = packed
    if lax.axis_size("gy") == 1:
        return first, last
    return line(first, "gy", -1), line(last, "gy", 1)


def lanes_z(packed):
    size = lax.axis_size("gz")
    if size == 1:
        return packed, packed
    if size == 2:
        other = ring(packed, "gz", 1)
        return other, other
    return ring(packed, "gz", -1), ring(packed, "gz", 1)


class Shifts:
    def __init__(self, rows, lanes):
        self.rows, self.lanes = rows, lanes
        self.row = lax.broadcasted_iota(jnp.int32, (rows, lanes), 0)
        self.lane = lax.broadcasted_iota(jnp.int32, (rows, lanes), 1)
        wall, walls = lax.axis_index("gy"), lax.axis_size("gy")
        self.last_wall = jnp.full((rows, lanes), wall, jnp.int32) == walls - 1
        self.first_wall = jnp.full((rows, lanes), wall, jnp.int32) == 0

    def edges(self, above_ref, below_ref, place):
        shape = (self.rows, self.lanes)
        above = jnp.broadcast_to(above_ref[pl.ds(place, 1), :], shape)
        below = jnp.broadcast_to(below_ref[pl.ds(place, 1), :], shape)
        return jnp.where(self.last_wall, 0.0, above), jnp.where(self.first_wall, 0.0, below)

    def y(self, plane, above, below):
        up = jnp.where(self.row == self.rows - 1, above, pltpu.roll(plane, self.rows - 1, 0))
        down = jnp.where(self.row == 0, below, pltpu.roll(plane, 1, 0))
        return up, down

    def z(self, plane, edge):
        up = pltpu.roll(jnp.where(self.lane == 0, edge, plane), self.lanes - 1, 1)
        down = pltpu.roll(jnp.where(self.lane == self.lanes - 1, edge, plane), 1, 1)
        return up, down


def stretch_pull(conf, dual, column):
    out = []
    for m in range(3):
        total = 0.0
        for j in range(3):
            term = dual[COMP[m][j]] * conf[COMP[j][column]]
            total = total + (term + term if j == m else term)
        out.append(total)
    return out


def half_factor(conf):
    return (0.5 * (EXTENSIBILITY - 3.0)) / (EXTENSIBILITY - (conf[0] + conf[1] + conf[2]))


def halo_planes(ref, start, count, offset, below_ref, above_ref):
    depth = ref.shape[1]
    fields = []
    for f in range(9):
        planes = []
        for p in range(start - 1, start + count + 1):
            if p < 0:
                planes.append(below_ref[offset + f])
            elif p == depth:
                planes.append(above_ref[offset + f])
            else:
                planes.append(ref[f, p])
        fields.append(planes)
    return fields


def raw_kernel(start, count, has_below, has_above, *refs):
    steps_ref, seed_ref, dual_ref, ya_ref, yb_ref, z_ref, *halo_refs, raw_ref = refs
    below_ref = halo_refs[0] if has_below else None
    above_ref = halo_refs[-1] if has_above else None
    _, depth, rows, lanes = seed_ref.shape
    shift = Shifts(rows, lanes)
    time_step = HORIZON / jnp.full((rows, lanes), steps_ref[0], jnp.int32).astype(jnp.float32)
    seed = halo_planes(seed_ref, start, count, 0, below_ref, above_ref)
    dual = halo_planes(dual_ref, start, count, 9, below_ref, above_ref)
    pull_x = [
        stretch_pull([c[p] for c in seed[3:]], [c[p] for c in dual[3:]], 0) for p in range(count + 2)
    ]
    for q in range(count):
        p, at = start + q, q + 1
        conf = [c[at] for c in seed[3:]]
        pulled = [c[at] for c in dual[3:]]
        seed_y = [shift.edges(ya_ref, yb_ref, f * depth + p) for f in range(9)]
        dual_y = [shift.edges(ya_ref, yb_ref, (9 + f) * depth + p) for f in range(9)]
        seed_z = [z_ref[f, p] for f in range(9)]
        dual_z = [z_ref[9 + f, p] for f in range(9)]
        laps, slopes = [], []
        for f in range(9):
            here = dual[f][at]
            yu, yd = shift.y(here, *dual_y[f])
            zu, zd = shift.z(here, dual_z[f])
            xu, xd = dual[f][at + 1], dual[f][at - 1]
            laps.append((xu + xd) + (yu + yd) + (zu + zd) - 6.0 * here)
            if f < 3:
                slopes.append((0.5 * (xu - xd), 0.5 * (yu - yd), 0.5 * (zu - zd)))
        grads = []
        for f in range(3):
            here = seed[f][at]
            yu, yd = shift.y(here, *seed_y[f])
            zu, zd = shift.z(here, seed_z[f])
            xu, xd = seed[f][at + 1], seed[f][at - 1]
            grads.append((0.5 * (xu - xd), 0.5 * (yu - yd), 0.5 * (zu - zd)))
        pull_y = stretch_pull(conf, pulled, 1)
        pull_z = stretch_pull(conf, pulled, 2)
        above_y = stretch_pull([c[0] for c in seed_y[3:]], [c[0] for c in dual_y[3:]], 1)
        below_y = stretch_pull([c[1] for c in seed_y[3:]], [c[1] for c in dual_y[3:]], 1)
        edge_z = stretch_pull(seed_z[3:], dual_z[3:], 2)
        for m in range(3):
            yu, yd = shift.y(pull_y[m], above_y[m], below_y[m])
            zu, zd = shift.z(pull_z[m], edge_z[m])
            flux = 0.5 * ((pull_x[at + 1][m] - pull_x[at - 1][m]) + (yu - yd) + (zu - zd))
            raw_ref[m, q] = dual[m][at] + time_step * (VISCOSITY * laps[m] - flux)
        half = half_factor(conf)
        stress = []
        for n, (i, j) in enumerate(PAIRS):
            slope = slopes[i][j] if i == j else slopes[i][j] + slopes[j][i]
            stress.append(-(slope + pulled[n]))
        inner = 0.0
        for n in range(6):
            inner = inner + stress[n] * conf[n]
        inner = inner * (half * half) * (2.0 / (EXTENSIBILITY - 3.0))

        def weight(k, j):
            total = 0.0
            for m in range(3):
                term = grads[m][k] * pulled[COMP[m][j]]
                total = total + (term + term if m == j else term)
            return total

        for n, (i, j) in enumerate(PAIRS):
            change = DIFFUSIVITY * laps[3 + n] + half * stress[n]
            change = change + (weight(i, i) + inner if i == j else weight(i, j) + weight(j, i))
            raw_ref[3 + n, q] = pulled[n] + time_step * change


def next_kernel(steps_ref, seed_ref, ya_ref, yb_ref, z_ref, below_ref, above_ref, next_ref):
    _, depth, rows, lanes = seed_ref.shape
    shift = Shifts(rows, lanes)
    time_step = HORIZON / jnp.full((rows, lanes), steps_ref[0], jnp.int32).astype(jnp.float32)
    seed = halo_planes(seed_ref, 0, depth, 0, below_ref, above_ref)
    halves = [half_factor([c[p] for c in seed[3:]]) for p in range(depth + 2)]
    for p in range(depth):
        at = p + 1
        conf = [c[at] for c in seed[3:]]
        ey = [shift.edges(ya_ref, yb_ref, f * depth + p) for f in range(9)]
        ez = [z_ref[f, p] for f in range(9)]
        laps, grads = [], []
        for f in range(9):
            here = seed[f][at]
            yu, yd = shift.y(here, *ey[f])
            zu, zd = shift.z(here, ez[f])
            xu, xd = seed[f][at + 1], seed[f][at - 1]
            laps.append((xu + xd) + (yu + yd) + (zu + zd) - 6.0 * here)
            if f < 3:
                grads.append((0.5 * (xu - xd), 0.5 * (yu - yd), 0.5 * (zu - zd)))
        half = halves[at]
        half_above, half_below = half_factor([c[0] for c in ey[3:]]), half_factor([c[1] for c in ey[3:]])
        half_z = half_factor(ez[3:])
        for i in range(3):
            cx, cy, cz = COMP[i]
            yu, yd = shift.y(half * conf[cy], half_above * ey[3 + cy][0], half_below * ey[3 + cy][1])
            zu, zd = shift.z(half * conf[cz], half_z * ez[3 + cz])
            xu = halves[at + 1] * seed[3 + cx][at + 1]
            xd = halves[at - 1] * seed[3 + cx][at - 1]
            divergence = 0.5 * ((xu - xd) + (yu - yd) + (zu - zd))
            next_ref[i, p] = seed[i][at] + time_step * (VISCOSITY * laps[i] + divergence)
        for n, (i, j) in enumerate(PAIRS):
            stretch = 0.0
            for k in range(3):
                term = grads[i][k] * conf[COMP[k][j]]
                stretch = stretch + (term + term if i == j else term + grads[j][k] * conf[COMP[k][i]])
            stress = half * conf[n] - (0.5 if i == j else 0.0)
            next_ref[3 + n, p] = conf[n] + time_step * (DIFFUSIVITY * laps[3 + n] + stretch - stress)


def average_kernel(*refs):
    *pairs, out_ref = refs
    plane = 0
    for raw_ref, image_ref in zip(pairs[::2], pairs[1::2]):
        for q in range(raw_ref.shape[1]):
            for f, sign in enumerate(SIGNS):
                raw, image = raw_ref[f, q], image_ref[f, q]
                out_ref[f, plane] = 0.5 * (raw + image if sign > 0 else raw - image)
            plane += 1


def call(kernel, shape, steps, *arrays):
    vmem = pl.BlockSpec(memory_space=pltpu.VMEM)
    scalars = [pl.BlockSpec(memory_space=pltpu.SMEM)] * len(steps)
    return pl.pallas_call(
        kernel,
        out_shape=jax.ShapeDtypeStruct(shape, jnp.float32),
        in_specs=scalars + [vmem] * len(arrays),
        out_specs=vmem,
        cost_estimate=estimate(1_000_000),
        compiler_params=grant(),
    )(*steps, *arrays)


def per_device(seed_state, costate, step_count):
    depth = seed_state.shape[1]
    first, last = (jnp.concatenate([x[:, p] for x in (seed_state, costate)], 0) for p in (0, -1))
    below = ring(last, "gx", 1)
    above = ring(first, "gx", -1)
    lanes, *rows = pack(seed_state, costate)
    ya, yb = rows_y(rows)
    z = call(unpack_kernel, (18,) + seed_state.shape[1:], (), *lanes_z(lanes))
    walls = lax.axis_size("gy")
    pairs = []
    for start, count in ((0, depth - 1), (depth - 1, 1)):
        if count == 0:
            continue
        has_below, has_above = start == 0, start + count == depth
        raw = call(
            functools.partial(raw_kernel, start, count, has_below, has_above),
            (9, count) + seed_state.shape[2:],
            (step_count,),
            *(seed_state, costate, ya, yb, z),
            *((below,) if has_below else ()),
            *((above,) if has_above else ()),
        )
        partner = lax.ppermute(raw, "gy", [(i, walls - 1 - i) for i in range(walls)])
        pairs += [raw, jnp.flip(partner, axis=2)]
    next_state = call(next_kernel, seed_state.shape, (step_count,), seed_state, ya, yb, z, below, above)
    return next_state, call(average_kernel, seed_state.shape, (), *pairs)


def solution(mesh):
    placed = P(None, ("rep", "gx"), "gy", "gz")
    return jax.shard_map(
        per_device,
        mesh=mesh,
        in_specs=(placed, placed, P("rep")),
        out_specs=(placed, placed),
        check_vma=False,
    )
```

```python
import functools

import jax
import jax.numpy as jnp
from jax import lax
from jax.experimental import pallas as pl
from jax.experimental.pallas import tpu as pltpu
from jax.sharding import PartitionSpec as P

VISCOSITY = 0.5
DIFFUSIVITY = 0.2
EXTENSIBILITY = 100.0
HORIZON = 1.0
COMP = ((0, 3, 4), (3, 1, 5), (4, 5, 2))
PAIRS = ((0, 0), (1, 1), (2, 2), (0, 1), (0, 2), (1, 2))
SIGNS = (1.0, -1.0, 1.0, 1.0, 1.0, 1.0, -1.0, 1.0, -1.0)


def ring(array, axis, step):
    size = lax.axis_size(axis)
    return lax.ppermute(array, axis, [(i, (i + step) % size) for i in range(size)])


def line(array, axis, step):
    size = lax.axis_size(axis)
    return lax.ppermute(array, axis, [(i, i + step) for i in range(size) if 0 <= i + step < size])


def pack_kernel(seed_ref, dual_ref, lanes_ref, *rows_refs):
    fields, depth, rows, lanes = seed_ref.shape
    half = lanes // 2
    if len(rows_refs) == 1:
        places = [jnp.where(lax.axis_index("gy") == 0, rows - 1, 0)]
    else:
        places = [0, rows - 1]
    lane = lax.broadcasted_iota(jnp.int32, (rows, lanes), 1)
    packed = [jnp.zeros((rows, lanes), jnp.float32)] * lanes_ref.shape[0]
    for f in range(2 * fields):
        ref = seed_ref if f < fields else dual_ref
        for p in range(depth):
            n = f * depth + p
            for place, rows_ref in zip(places, rows_refs):
                rows_ref[pl.ds(n, 1), :] = ref[f % fields, p, pl.ds(place, 1), :]
            group, slot = divmod(n, half)
            plane = ref[f % fields, p]
            first = turned(plane, slot)
            last = turned(plane, half + slot + 1 - lanes)
            packed[group] = jnp.where(lane == slot, first, jnp.where(lane == half + slot, last, packed[group]))
    for group, plane in enumerate(packed):
        lanes_ref[group] = plane


def unpack_kernel(above_ref, below_ref, edges_ref):
    fields, depth, rows, lanes = edges_ref.shape
    half = lanes // 2
    lane = lax.broadcasted_iota(jnp.int32, (rows, lanes), 1)
    for f in range(fields):
        for p in range(depth):
            group, slot = divmod(f * depth + p, half)
            above = turned(above_ref[group], -slot)
            below = turned(below_ref[group], lanes - 1 - half - slot)
            edges_ref[f, p] = jnp.where(lane < half, above, below)


def turned(plane, step):
    step = step % plane.shape[1]
    return pltpu.roll(plane, step, 1) if step else plane


def estimate(bytes_accessed):
    return pl.CostEstimate(flops=1_000_000, bytes_accessed=bytes_accessed, transcendentals=0)


def grant():
    return pltpu.CompilerParams(vmem_limit_bytes=16 * 1024 * 1024)


def pack(seed_state, costate):
    fields, depth, rows, lanes = seed_state.shape
    count = 2 * fields * depth
    groups = -(-count // (lanes // 2))
    vmem = pl.BlockSpec(memory_space=pltpu.VMEM)
    shapes = [jax.ShapeDtypeStruct((groups, rows, lanes), jnp.float32)]
    shapes += [jax.ShapeDtypeStruct((count, lanes), jnp.float32)] * (1 if lax.axis_size("gy") == 2 else 2)
    return pl.pallas_call(
        pack_kernel,
        out_shape=shapes,
        in_specs=[vmem] * 2,
        out_specs=[vmem] * len(shapes),
        cost_estimate=estimate(300_000),
        compiler_params=grant(),
    )(seed_state, costate)


def rows_y(packed):
    if len(packed) == 1:
        other = ring(packed[0], "gy", 1)
        return other, other
    first, last = packed
    if lax.axis_size("gy") == 1:
        return first, last
    return line(first, "gy", -1), line(last, "gy", 1)


def lanes_z(packed):
    size = lax.axis_size("gz")
    if size == 1:
        return packed, packed
    if size == 2:
        other = ring(packed, "gz", 1)
        return other, other
    return ring(packed, "gz", -1), ring(packed, "gz", 1)


class Shifts:
    def __init__(self, rows, lanes):
        self.rows, self.lanes = rows, lanes
        self.row = lax.broadcasted_iota(jnp.int32, (rows, lanes), 0)
        self.lane = lax.broadcasted_iota(jnp.int32, (rows, lanes), 1)
        wall, walls = lax.axis_index("gy"), lax.axis_size("gy")
        self.last_wall = jnp.full((rows, lanes), wall, jnp.int32) == walls - 1
        self.first_wall = jnp.full((rows, lanes), wall, jnp.int32) == 0

    def edges(self, above_ref, below_ref, place):
        shape = (self.rows, self.lanes)
        above = jnp.broadcast_to(above_ref[pl.ds(place, 1), :], shape)
        below = jnp.broadcast_to(below_ref[pl.ds(place, 1), :], shape)
        return jnp.where(self.last_wall, 0.0, above), jnp.where(self.first_wall, 0.0, below)

    def y(self, plane, above, below):
        up = jnp.where(self.row == self.rows - 1, above, pltpu.roll(plane, self.rows - 1, 0))
        down = jnp.where(self.row == 0, below, pltpu.roll(plane, 1, 0))
        return up, down

    def z(self, plane, edge):
        up = pltpu.roll(jnp.where(self.lane == 0, edge, plane), self.lanes - 1, 1)
        down = pltpu.roll(jnp.where(self.lane == self.lanes - 1, edge, plane), 1, 1)
        return up, down


def stretch_pull(conf, dual, column):
    out = []
    for m in range(3):
        total = 0.0
        for j in range(3):
            term = dual[COMP[m][j]] * conf[COMP[j][column]]
            total = total + (term + term if j == m else term)
        out.append(total)
    return out


def half_factor(conf):
    return (0.5 * (EXTENSIBILITY - 3.0)) / (EXTENSIBILITY - (conf[0] + conf[1] + conf[2]))


def halo_planes(ref, below, above):
    depth = ref.shape[1]
    return [[below[f]] + [ref[f, p] for p in range(depth)] + [above[f]] for f in range(9)]


def local_kernel(*refs):
    steps_ref, seed_ref, dual_ref, ya_ref, yb_ref, z_ref, raw_ref = refs
    _, depth, rows, lanes = seed_ref.shape
    shift = Shifts(rows, lanes)
    time_step = HORIZON / jnp.full((rows, lanes), steps_ref[0], jnp.int32).astype(jnp.float32)
    nothing = [jnp.zeros((rows, lanes), jnp.float32)] * 9
    seed = halo_planes(seed_ref, nothing, nothing)
    dual = halo_planes(dual_ref, nothing, nothing)
    pull_x = [stretch_pull([c[p] for c in seed[3:]], [c[p] for c in dual[3:]], 0) for p in range(depth + 2)]
    for p in range(depth):
        at = p + 1
        conf = [c[at] for c in seed[3:]]
        pulled = [c[at] for c in dual[3:]]
        seed_y = [shift.edges(ya_ref, yb_ref, f * depth + p) for f in range(9)]
        dual_y = [shift.edges(ya_ref, yb_ref, (9 + f) * depth + p) for f in range(9)]
        seed_z = [z_ref[f, p] for f in range(9)]
        dual_z = [z_ref[9 + f, p] for f in range(9)]
        laps, slopes = [], []
        for f in range(9):
            here = dual[f][at]
            yu, yd = shift.y(here, *dual_y[f])
            zu, zd = shift.z(here, dual_z[f])
            xu, xd = dual[f][at + 1], dual[f][at - 1]
            laps.append((xu + xd) + (yu + yd) + (zu + zd) - 6.0 * here)
            if f < 3:
                slopes.append((0.5 * (xu - xd), 0.5 * (yu - yd), 0.5 * (zu - zd)))
        grads = []
        for f in range(3):
            here = seed[f][at]
            yu, yd = shift.y(here, *seed_y[f])
            zu, zd = shift.z(here, seed_z[f])
            xu, xd = seed[f][at + 1], seed[f][at - 1]
            grads.append((0.5 * (xu - xd), 0.5 * (yu - yd), 0.5 * (zu - zd)))
        pull_y = stretch_pull(conf, pulled, 1)
        pull_z = stretch_pull(conf, pulled, 2)
        above_y = stretch_pull([c[0] for c in seed_y[3:]], [c[0] for c in dual_y[3:]], 1)
        below_y = stretch_pull([c[1] for c in seed_y[3:]], [c[1] for c in dual_y[3:]], 1)
        edge_z = stretch_pull(seed_z[3:], dual_z[3:], 2)
        for m in range(3):
            yu, yd = shift.y(pull_y[m], above_y[m], below_y[m])
            zu, zd = shift.z(pull_z[m], edge_z[m])
            flux = 0.5 * ((pull_x[at + 1][m] - pull_x[at - 1][m]) + (yu - yd) + (zu - zd))
            raw_ref[m, p] = dual[m][at] + time_step * (VISCOSITY * laps[m] - flux)
        half = half_factor(conf)
        stress = []
        for n, (i, j) in enumerate(PAIRS):
            slope = slopes[i][j] if i == j else slopes[i][j] + slopes[j][i]
            stress.append(-(slope + pulled[n]))
        inner = 0.0
        for n in range(6):
            inner = inner + stress[n] * conf[n]
        inner = inner * (half * half) * (2.0 / (EXTENSIBILITY - 3.0))

        def weight(k, j):
            total = 0.0
            for m in range(3):
                term = grads[m][k] * pulled[COMP[m][j]]
                total = total + (term + term if m == j else term)
            return total

        for n, (i, j) in enumerate(PAIRS):
            change = DIFFUSIVITY * laps[3 + n] + half * stress[n]
            change = change + (weight(i, i) + inner if i == j else weight(i, j) + weight(j, i))
            raw_ref[3 + n, p] = pulled[n] + time_step * change


def add_halo(raw, side, time_step, seed_ref, dual_ref, plane, halo_ref):
    half_side = 0.5 * side
    speed = [halo_ref[f] for f in range(3)]
    flow = [halo_ref[9 + f] for f in range(3)]
    dual = [halo_ref[12 + f] for f in range(6)]
    pull = stretch_pull([halo_ref[3 + f] for f in range(6)], dual, 0)
    for m in range(3):
        raw[m] = raw[m] + time_step * (VISCOSITY * flow[m] - half_side * pull[m])
    conf = [seed_ref[3 + f, plane] for f in range(6)]
    pulled = [dual_ref[3 + f, plane] for f in range(6)]
    half = half_factor(conf)
    inner = 0.0
    for j in range(3):
        inner = inner + flow[j] * conf[COMP[0][j]]
    inner = inner * (half * half) * (-half_side * 2.0 / (EXTENSIBILITY - 3.0))
    for n, (i, j) in enumerate(PAIRS):
        change = DIFFUSIVITY * dual[n]
        if i == j:
            change = change + inner
        if i == 0:
            weight = 0.0
            for m in range(3):
                term = speed[m] * pulled[COMP[m][j]]
                weight = weight + (term + term if m == j else term)
            change = change + half_side * (weight - half * flow[j])
        raw[3 + n] = raw[3 + n] + time_step * change


def raw_kernel(start, count, has_below, has_above, *refs):
    steps_ref, seed_ref, dual_ref, local_ref, *halo_refs, raw_ref = refs
    _, depth, rows, lanes = seed_ref.shape
    time_step = HORIZON / jnp.full((rows, lanes), steps_ref[0], jnp.int32).astype(jnp.float32)
    for q in range(count):
        p = start + q
        raw = [local_ref[f, p] for f in range(9)]
        if p == 0 and has_below:
            add_halo(raw, -1.0, time_step, seed_ref, dual_ref, p, halo_refs[0])
        if p == depth - 1 and has_above:
            add_halo(raw, 1.0, time_step, seed_ref, dual_ref, p, halo_refs[-1])
        for f in range(9):
            raw_ref[f, q] = raw[f]


def next_kernel(steps_ref, seed_ref, ya_ref, yb_ref, z_ref, below_ref, above_ref, next_ref):
    _, depth, rows, lanes = seed_ref.shape
    shift = Shifts(rows, lanes)
    time_step = HORIZON / jnp.full((rows, lanes), steps_ref[0], jnp.int32).astype(jnp.float32)
    seed = halo_planes(seed_ref, [below_ref[f] for f in range(9)], [above_ref[f] for f in range(9)])
    halves = [half_factor([c[p] for c in seed[3:]]) for p in range(depth + 2)]
    for p in range(depth):
        at = p + 1
        conf = [c[at] for c in seed[3:]]
        ey = [shift.edges(ya_ref, yb_ref, f * depth + p) for f in range(9)]
        ez = [z_ref[f, p] for f in range(9)]
        laps, grads = [], []
        for f in range(9):
            here = seed[f][at]
            yu, yd = shift.y(here, *ey[f])
            zu, zd = shift.z(here, ez[f])
            xu, xd = seed[f][at + 1], seed[f][at - 1]
            laps.append((xu + xd) + (yu + yd) + (zu + zd) - 6.0 * here)
            if f < 3:
                grads.append((0.5 * (xu - xd), 0.5 * (yu - yd), 0.5 * (zu - zd)))
        half = halves[at]
        half_above, half_below = half_factor([c[0] for c in ey[3:]]), half_factor([c[1] for c in ey[3:]])
        half_z = half_factor(ez[3:])
        for i in range(3):
            cx, cy, cz = COMP[i]
            yu, yd = shift.y(half * conf[cy], half_above * ey[3 + cy][0], half_below * ey[3 + cy][1])
            zu, zd = shift.z(half * conf[cz], half_z * ez[3 + cz])
            xu = halves[at + 1] * seed[3 + cx][at + 1]
            xd = halves[at - 1] * seed[3 + cx][at - 1]
            divergence = 0.5 * ((xu - xd) + (yu - yd) + (zu - zd))
            next_ref[i, p] = seed[i][at] + time_step * (VISCOSITY * laps[i] + divergence)
        for n, (i, j) in enumerate(PAIRS):
            stretch = 0.0
            for k in range(3):
                term = grads[i][k] * conf[COMP[k][j]]
                stretch = stretch + (term + term if i == j else term + grads[j][k] * conf[COMP[k][i]])
            stress = half * conf[n] - (0.5 if i == j else 0.0)
            next_ref[3 + n, p] = conf[n] + time_step * (DIFFUSIVITY * laps[3 + n] + stretch - stress)


def average_kernel(*refs):
    *pairs, out_ref = refs
    plane = 0
    for raw_ref, image_ref in zip(pairs[::2], pairs[1::2]):
        for q in range(raw_ref.shape[1]):
            for f, sign in enumerate(SIGNS):
                raw, image = raw_ref[f, q], image_ref[f, q]
                out_ref[f, plane] = 0.5 * (raw + image if sign > 0 else raw - image)
            plane += 1


def call(kernel, shape, steps, *arrays):
    vmem = pl.BlockSpec(memory_space=pltpu.VMEM)
    scalars = [pl.BlockSpec(memory_space=pltpu.SMEM)] * len(steps)
    return pl.pallas_call(
        kernel,
        out_shape=jax.ShapeDtypeStruct(shape, jnp.float32),
        in_specs=scalars + [vmem] * len(arrays),
        out_specs=vmem,
        cost_estimate=estimate(1_000_000),
        compiler_params=grant(),
    )(*steps, *arrays)


def per_device(seed_state, costate, step_count):
    depth = seed_state.shape[1]
    first, last = (jnp.concatenate([x[:, p] for x in (seed_state, costate)], 0) for p in (0, -1))
    below = ring(last, "gx", 1)
    above = ring(first, "gx", -1)
    lanes, *rows = pack(seed_state, costate)
    ya, yb = rows_y(rows)
    z = call(unpack_kernel, (18,) + seed_state.shape[1:], (), *lanes_z(lanes))
    local = call(local_kernel, seed_state.shape, (step_count,), seed_state, costate, ya, yb, z)
    walls = lax.axis_size("gy")
    pairs = []
    for start, count in ((0, depth - 1), (depth - 1, 1)):
        if count == 0:
            continue
        has_below, has_above = start == 0, start + count == depth
        raw = call(
            functools.partial(raw_kernel, start, count, has_below, has_above),
            (9, count) + seed_state.shape[2:],
            (step_count,),
            *(seed_state, costate, local),
            *((below,) if has_below else ()),
            *((above,) if has_above else ()),
        )
        partner = lax.ppermute(raw, "gy", [(i, walls - 1 - i) for i in range(walls)])
        pairs += [raw, jnp.flip(partner, axis=2)]
    next_state = call(next_kernel, seed_state.shape, (step_count,), seed_state, ya, yb, z, below, above)
    return next_state, call(average_kernel, seed_state.shape, (), *pairs)


def solution(mesh):
    placed = P(None, ("rep", "gx"), "gy", "gz")
    return jax.shard_map(
        per_device,
        mesh=mesh,
        in_specs=(placed, placed, P("rep")),
        out_specs=(placed, placed),
        check_vma=False,
    )
```

```python
import functools

import jax
import jax.numpy as jnp
from jax import lax
from jax.experimental import pallas as pl
from jax.experimental.pallas import tpu as pltpu
from jax.sharding import PartitionSpec as P

VISCOSITY = 0.5
DIFFUSIVITY = 0.2
EXTENSIBILITY = 100.0
HORIZON = 1.0
COMP = ((0, 3, 4), (3, 1, 5), (4, 5, 2))
PAIRS = ((0, 0), (1, 1), (2, 2), (0, 1), (0, 2), (1, 2))
SIGNS = (1.0, -1.0, 1.0, 1.0, 1.0, 1.0, -1.0, 1.0, -1.0)


def ring(array, axis, step):
    size = lax.axis_size(axis)
    return lax.ppermute(array, axis, [(i, (i + step) % size) for i in range(size)])


def line(array, axis, step):
    size = lax.axis_size(axis)
    return lax.ppermute(array, axis, [(i, i + step) for i in range(size) if 0 <= i + step < size])


def pack_kernel(seed_ref, dual_ref, lanes_ref, *rows_refs):
    fields, depth, rows, lanes = seed_ref.shape
    half = lanes // 2
    if len(rows_refs) == 1:
        places = [jnp.where(lax.axis_index("gy") == 0, rows - 1, 0)]
    else:
        places = [0, rows - 1]
    lane = lax.broadcasted_iota(jnp.int32, (rows, lanes), 1)
    packed = [jnp.zeros((rows, lanes), jnp.float32)] * lanes_ref.shape[0]
    for f in range(2 * fields):
        ref = seed_ref if f < fields else dual_ref
        for p in range(depth):
            n = f * depth + p
            for place, rows_ref in zip(places, rows_refs):
                rows_ref[pl.ds(n, 1), :] = ref[f % fields, p, pl.ds(place, 1), :]
            group, slot = divmod(n, half)
            plane = ref[f % fields, p]
            first = turned(plane, slot)
            last = turned(plane, half + slot + 1 - lanes)
            packed[group] = jnp.where(lane == slot, first, jnp.where(lane == half + slot, last, packed[group]))
    for group, plane in enumerate(packed):
        lanes_ref[group] = plane


def unpack_kernel(above_ref, below_ref, edges_ref):
    fields, depth, rows, lanes = edges_ref.shape
    half = lanes // 2
    lane = lax.broadcasted_iota(jnp.int32, (rows, lanes), 1)
    for f in range(fields):
        for p in range(depth):
            group, slot = divmod(f * depth + p, half)
            above = turned(above_ref[group], -slot)
            below = turned(below_ref[group], lanes - 1 - half - slot)
            edges_ref[f, p] = jnp.where(lane < half, above, below)


def turned(plane, step):
    step = step % plane.shape[1]
    return pltpu.roll(plane, step, 1) if step else plane


def estimate(bytes_accessed):
    return pl.CostEstimate(flops=1_000_000, bytes_accessed=bytes_accessed, transcendentals=0)


def grant():
    return pltpu.CompilerParams(vmem_limit_bytes=16 * 1024 * 1024)


def pack(seed_state, costate):
    fields, depth, rows, lanes = seed_state.shape
    count = 2 * fields * depth
    groups = -(-count // (lanes // 2))
    vmem = pl.BlockSpec(memory_space=pltpu.VMEM)
    shapes = [jax.ShapeDtypeStruct((groups, rows, lanes), jnp.float32)]
    shapes += [jax.ShapeDtypeStruct((count, lanes), jnp.float32)] * (1 if lax.axis_size("gy") == 2 else 2)
    return pl.pallas_call(
        pack_kernel,
        out_shape=shapes,
        in_specs=[vmem] * 2,
        out_specs=[vmem] * len(shapes),
        cost_estimate=estimate(300_000),
        compiler_params=grant(),
    )(seed_state, costate)


def rows_y(packed):
    if len(packed) == 1:
        other = ring(packed[0], "gy", 1)
        return other, other
    first, last = packed
    if lax.axis_size("gy") == 1:
        return first, last
    return line(first, "gy", -1), line(last, "gy", 1)


def lanes_z(packed):
    size = lax.axis_size("gz")
    if size == 1:
        return packed, packed
    if size == 2:
        other = ring(packed, "gz", 1)
        return other, other
    return ring(packed, "gz", -1), ring(packed, "gz", 1)


class Shifts:
    def __init__(self, rows, lanes):
        self.rows, self.lanes = rows, lanes
        self.row = lax.broadcasted_iota(jnp.int32, (rows, lanes), 0)
        self.lane = lax.broadcasted_iota(jnp.int32, (rows, lanes), 1)
        wall, walls = lax.axis_index("gy"), lax.axis_size("gy")
        self.last_wall = jnp.full((rows, lanes), wall, jnp.int32) == walls - 1
        self.first_wall = jnp.full((rows, lanes), wall, jnp.int32) == 0

    def edges(self, above_ref, below_ref, place):
        shape = (self.rows, self.lanes)
        above = jnp.broadcast_to(above_ref[pl.ds(place, 1), :], shape)
        below = jnp.broadcast_to(below_ref[pl.ds(place, 1), :], shape)
        return jnp.where(self.last_wall, 0.0, above), jnp.where(self.first_wall, 0.0, below)

    def y(self, plane, above, below):
        up = jnp.where(self.row == self.rows - 1, above, pltpu.roll(plane, self.rows - 1, 0))
        down = jnp.where(self.row == 0, below, pltpu.roll(plane, 1, 0))
        return up, down

    def z(self, plane, edge):
        up = pltpu.roll(jnp.where(self.lane == 0, edge, plane), self.lanes - 1, 1)
        down = pltpu.roll(jnp.where(self.lane == self.lanes - 1, edge, plane), 1, 1)
        return up, down


def stretch_pull(conf, dual, column):
    out = []
    for m in range(3):
        total = 0.0
        for j in range(3):
            term = dual[COMP[m][j]] * conf[COMP[j][column]]
            total = total + (term + term if j == m else term)
        out.append(total)
    return out


def half_factor(conf):
    return (0.5 * (EXTENSIBILITY - 3.0)) / (EXTENSIBILITY - (conf[0] + conf[1] + conf[2]))


def halo_planes(ref, below, above):
    depth = ref.shape[1]
    return [[below[f]] + [ref[f, p] for p in range(depth)] + [above[f]] for f in range(9)]


def local_kernel(*refs):
    steps_ref, seed_ref, dual_ref, ya_ref, yb_ref, z_ref, raw_ref = refs
    _, depth, rows, lanes = seed_ref.shape
    shift = Shifts(rows, lanes)
    time_step = HORIZON / jnp.full((rows, lanes), steps_ref[0], jnp.int32).astype(jnp.float32)
    nothing = [jnp.zeros((rows, lanes), jnp.float32)] * 9
    seed = halo_planes(seed_ref, nothing, nothing)
    dual = halo_planes(dual_ref, nothing, nothing)
    pull_x = [stretch_pull([c[p] for c in seed[3:]], [c[p] for c in dual[3:]], 0) for p in range(depth + 2)]
    for p in range(depth):
        at = p + 1
        conf = [c[at] for c in seed[3:]]
        pulled = [c[at] for c in dual[3:]]
        seed_y = [shift.edges(ya_ref, yb_ref, f * depth + p) for f in range(9)]
        dual_y = [shift.edges(ya_ref, yb_ref, (9 + f) * depth + p) for f in range(9)]
        seed_z = [z_ref[f, p] for f in range(9)]
        dual_z = [z_ref[9 + f, p] for f in range(9)]
        laps, slopes = [], []
        for f in range(9):
            here = dual[f][at]
            yu, yd = shift.y(here, *dual_y[f])
            zu, zd = shift.z(here, dual_z[f])
            xu, xd = dual[f][at + 1], dual[f][at - 1]
            laps.append((xu + xd) + (yu + yd) + (zu + zd) - 6.0 * here)
            if f < 3:
                slopes.append((0.5 * (xu - xd), 0.5 * (yu - yd), 0.5 * (zu - zd)))
        grads = []
        for f in range(3):
            here = seed[f][at]
            yu, yd = shift.y(here, *seed_y[f])
            zu, zd = shift.z(here, seed_z[f])
            xu, xd = seed[f][at + 1], seed[f][at - 1]
            grads.append((0.5 * (xu - xd), 0.5 * (yu - yd), 0.5 * (zu - zd)))
        pull_y = stretch_pull(conf, pulled, 1)
        pull_z = stretch_pull(conf, pulled, 2)
        above_y = stretch_pull([c[0] for c in seed_y[3:]], [c[0] for c in dual_y[3:]], 1)
        below_y = stretch_pull([c[1] for c in seed_y[3:]], [c[1] for c in dual_y[3:]], 1)
        edge_z = stretch_pull(seed_z[3:], dual_z[3:], 2)
        for m in range(3):
            yu, yd = shift.y(pull_y[m], above_y[m], below_y[m])
            zu, zd = shift.z(pull_z[m], edge_z[m])
            flux = 0.5 * ((pull_x[at + 1][m] - pull_x[at - 1][m]) + (yu - yd) + (zu - zd))
            raw_ref[m, p] = dual[m][at] + time_step * (VISCOSITY * laps[m] - flux)
        half = half_factor(conf)
        stress = []
        for n, (i, j) in enumerate(PAIRS):
            slope = slopes[i][j] if i == j else slopes[i][j] + slopes[j][i]
            stress.append(-(slope + pulled[n]))
        inner = 0.0
        for n in range(6):
            inner = inner + stress[n] * conf[n]
        inner = inner * (half * half) * (2.0 / (EXTENSIBILITY - 3.0))

        def weight(k, j):
            total = 0.0
            for m in range(3):
                term = grads[m][k] * pulled[COMP[m][j]]
                total = total + (term + term if m == j else term)
            return total

        for n, (i, j) in enumerate(PAIRS):
            change = DIFFUSIVITY * laps[3 + n] + half * stress[n]
            change = change + (weight(i, i) + inner if i == j else weight(i, j) + weight(j, i))
            raw_ref[3 + n, p] = pulled[n] + time_step * change


def add_halo(raw, side, time_step, seed_ref, dual_ref, plane, halo_ref):
    half_side = 0.5 * side
    speed = [halo_ref[f] for f in range(3)]
    flow = [halo_ref[9 + f] for f in range(3)]
    dual = [halo_ref[12 + f] for f in range(6)]
    pull = stretch_pull([halo_ref[3 + f] for f in range(6)], dual, 0)
    for m in range(3):
        raw[m] = raw[m] + time_step * (VISCOSITY * flow[m] - half_side * pull[m])
    conf = [seed_ref[3 + f, plane] for f in range(6)]
    pulled = [dual_ref[3 + f, plane] for f in range(6)]
    half = half_factor(conf)
    inner = 0.0
    for j in range(3):
        inner = inner + flow[j] * conf[COMP[0][j]]
    inner = inner * (half * half) * (-half_side * 2.0 / (EXTENSIBILITY - 3.0))
    for n, (i, j) in enumerate(PAIRS):
        change = DIFFUSIVITY * dual[n]
        if i == j:
            change = change + inner
        if i == 0:
            weight = 0.0
            for m in range(3):
                term = speed[m] * pulled[COMP[m][j]]
                weight = weight + (term + term if m == j else term)
            change = change + half_side * (weight - half * flow[j])
        raw[3 + n] = raw[3 + n] + time_step * change


def raw_kernel(start, count, has_below, has_above, *refs):
    steps_ref, seed_ref, dual_ref, local_ref, *halo_refs, raw_ref = refs
    _, depth, rows, lanes = seed_ref.shape
    time_step = HORIZON / jnp.full((rows, lanes), steps_ref[0], jnp.int32).astype(jnp.float32)
    for q in range(count):
        p = start + q
        raw = [local_ref[f, p] for f in range(9)]
        if p == 0 and has_below:
            add_halo(raw, -1.0, time_step, seed_ref, dual_ref, p, halo_refs[0])
        if p == depth - 1 and has_above:
            add_halo(raw, 1.0, time_step, seed_ref, dual_ref, p, halo_refs[-1])
        for f in range(9):
            raw_ref[f, q] = raw[f]


def next_kernel(steps_ref, seed_ref, ya_ref, yb_ref, z_ref, below_ref, above_ref, next_ref):
    _, depth, rows, lanes = seed_ref.shape
    shift = Shifts(rows, lanes)
    time_step = HORIZON / jnp.full((rows, lanes), steps_ref[0], jnp.int32).astype(jnp.float32)
    seed = halo_planes(seed_ref, [below_ref[f] for f in range(9)], [above_ref[f] for f in range(9)])
    halves = [half_factor([c[p] for c in seed[3:]]) for p in range(depth + 2)]
    for p in range(depth):
        at = p + 1
        conf = [c[at] for c in seed[3:]]
        ey = [shift.edges(ya_ref, yb_ref, f * depth + p) for f in range(9)]
        ez = [z_ref[f, p] for f in range(9)]
        laps, grads = [], []
        for f in range(9):
            here = seed[f][at]
            yu, yd = shift.y(here, *ey[f])
            zu, zd = shift.z(here, ez[f])
            xu, xd = seed[f][at + 1], seed[f][at - 1]
            laps.append((xu + xd) + (yu + yd) + (zu + zd) - 6.0 * here)
            if f < 3:
                grads.append((0.5 * (xu - xd), 0.5 * (yu - yd), 0.5 * (zu - zd)))
        half = halves[at]
        half_above, half_below = half_factor([c[0] for c in ey[3:]]), half_factor([c[1] for c in ey[3:]])
        half_z = half_factor(ez[3:])
        for i in range(3):
            cx, cy, cz = COMP[i]
            yu, yd = shift.y(half * conf[cy], half_above * ey[3 + cy][0], half_below * ey[3 + cy][1])
            zu, zd = shift.z(half * conf[cz], half_z * ez[3 + cz])
            xu = halves[at + 1] * seed[3 + cx][at + 1]
            xd = halves[at - 1] * seed[3 + cx][at - 1]
            divergence = 0.5 * ((xu - xd) + (yu - yd) + (zu - zd))
            next_ref[i, p] = seed[i][at] + time_step * (VISCOSITY * laps[i] + divergence)
        for n, (i, j) in enumerate(PAIRS):
            stretch = 0.0
            for k in range(3):
                term = grads[i][k] * conf[COMP[k][j]]
                stretch = stretch + (term + term if i == j else term + grads[j][k] * conf[COMP[k][i]])
            stress = half * conf[n] - (0.5 if i == j else 0.0)
            next_ref[3 + n, p] = conf[n] + time_step * (DIFFUSIVITY * laps[3 + n] + stretch - stress)


def average_kernel(planes, *refs):
    raw_ref, image_ref, *_, out_ref, mean_ref, sem = refs
    for f, sign in enumerate(SIGNS):
        for q in range(raw_ref.shape[1]):
            raw, image = raw_ref[f, q], image_ref[f, q]
            mean_ref[f, q] = 0.5 * (raw + image if sign > 0 else raw - image)
    copy = pltpu.make_async_copy(mean_ref, out_ref.at[:, planes], sem)
    copy.start()
    copy.wait()


def average(start, shape, raw, image, so_far):
    vmem = pl.BlockSpec(memory_space=pltpu.VMEM)
    hbm = pl.BlockSpec(memory_space=pltpu.HBM)
    earlier = () if so_far is None else (so_far,)
    return pl.pallas_call(
        functools.partial(average_kernel, pl.ds(start, raw.shape[1])),
        out_shape=jax.ShapeDtypeStruct(shape, jnp.float32),
        in_specs=[vmem] * 2 + [hbm] * len(earlier),
        out_specs=hbm,
        scratch_shapes=[pltpu.VMEM(raw.shape, jnp.float32), pltpu.SemaphoreType.DMA],
        input_output_aliases={2: 0} if earlier else {},
        cost_estimate=estimate(1_000_000),
        compiler_params=grant(),
    )(raw, image, *earlier)


def call(kernel, shape, steps, *arrays):
    vmem = pl.BlockSpec(memory_space=pltpu.VMEM)
    scalars = [pl.BlockSpec(memory_space=pltpu.SMEM)] * len(steps)
    return pl.pallas_call(
        kernel,
        out_shape=jax.ShapeDtypeStruct(shape, jnp.float32),
        in_specs=scalars + [vmem] * len(arrays),
        out_specs=vmem,
        cost_estimate=estimate(1_000_000),
        compiler_params=grant(),
    )(*steps, *arrays)


def per_device(seed_state, costate, step_count):
    depth = seed_state.shape[1]
    first, last = (jnp.concatenate([x[:, p] for x in (seed_state, costate)], 0) for p in (0, -1))
    below = ring(last, "gx", 1)
    above = ring(first, "gx", -1)
    lanes, *rows = pack(seed_state, costate)
    ya, yb = rows_y(rows)
    z = call(unpack_kernel, (18,) + seed_state.shape[1:], (), *lanes_z(lanes))
    local = call(local_kernel, seed_state.shape, (step_count,), seed_state, costate, ya, yb, z)
    walls = lax.axis_size("gy")
    gradient = None
    for start, count in ((0, depth - 1), (depth - 1, 1)):
        if count == 0:
            continue
        has_below, has_above = start == 0, start + count == depth
        raw = call(
            functools.partial(raw_kernel, start, count, has_below, has_above),
            (9, count) + seed_state.shape[2:],
            (step_count,),
            *(seed_state, costate, local),
            *((below,) if has_below else ()),
            *((above,) if has_above else ()),
        )
        partner = lax.ppermute(raw, "gy", [(i, walls - 1 - i) for i in range(walls)])
        gradient = average(start, seed_state.shape, raw, jnp.flip(partner, axis=2), gradient)
    next_state = call(next_kernel, seed_state.shape, (step_count,), seed_state, ya, yb, z, below, above)
    return next_state, gradient


def solution(mesh):
    placed = P(None, ("rep", "gx"), "gy", "gz")
    return jax.shard_map(
        per_device,
        mesh=mesh,
        in_specs=(placed, placed, P("rep")),
        out_specs=(placed, placed),
        check_vma=False,
    )
```

```python
import functools

import jax
import jax.numpy as jnp
from jax import lax
from jax.experimental import pallas as pl
from jax.experimental.pallas import tpu as pltpu
from jax.sharding import PartitionSpec as P

VISCOSITY = 0.5
DIFFUSIVITY = 0.2
EXTENSIBILITY = 100.0
HORIZON = 1.0
COMP = ((0, 3, 4), (3, 1, 5), (4, 5, 2))
PAIRS = ((0, 0), (1, 1), (2, 2), (0, 1), (0, 2), (1, 2))
SIGNS = (1.0, -1.0, 1.0, 1.0, 1.0, 1.0, -1.0, 1.0, -1.0)


def ring(array, axis, step):
    size = lax.axis_size(axis)
    return lax.ppermute(array, axis, [(i, (i + step) % size) for i in range(size)])


def line(array, axis, step):
    size = lax.axis_size(axis)
    return lax.ppermute(array, axis, [(i, i + step) for i in range(size) if 0 <= i + step < size])


def faces_kernel(seed_ref, dual_ref, first_ref, last_ref, sems):
    fields, depth = seed_ref.shape[:2]
    for n, (plane, face_ref) in enumerate(((depth - 1, last_ref), (0, first_ref))):
        for m, ref in enumerate((seed_ref, dual_ref)):
            for f in range(fields):
                pltpu.make_async_copy(ref.at[f, plane], face_ref.at[m * fields + f], sems.at[n]).start()
    for n, face_ref in enumerate((last_ref, first_ref)):
        pltpu.make_async_copy(face_ref, face_ref, sems.at[n]).wait()


def faces(seed_state, costate):
    fields, _, rows, lanes = seed_state.shape
    vmem = pl.BlockSpec(memory_space=pltpu.VMEM)
    return pl.pallas_call(
        faces_kernel,
        out_shape=[jax.ShapeDtypeStruct((2 * fields, rows, lanes), jnp.float32)] * 2,
        in_specs=[pl.BlockSpec(memory_space=pltpu.HBM)] * 2,
        out_specs=[vmem] * 2,
        scratch_shapes=[pltpu.SemaphoreType.DMA((2,))],
        cost_estimate=estimate(600_000),
        compiler_params=grant(),
    )(*(pltpu.with_memory_space_constraint(x, pltpu.HBM) for x in (seed_state, costate)))


def pack_kernel(seed_ref, dual_ref, lanes_ref, *rows_refs):
    fields, depth, rows, lanes = seed_ref.shape
    half = lanes // 2
    if len(rows_refs) == 1:
        places = [jnp.where(lax.axis_index("gy") == 0, rows - 1, 0)]
    else:
        places = [0, rows - 1]
    lane = lax.broadcasted_iota(jnp.int32, (rows, lanes), 1)
    packed = [jnp.zeros((rows, lanes), jnp.float32)] * lanes_ref.shape[0]
    for f in range(2 * fields):
        ref = seed_ref if f < fields else dual_ref
        for p in range(depth):
            n = f * depth + p
            for place, rows_ref in zip(places, rows_refs):
                rows_ref[pl.ds(n, 1), :] = ref[f % fields, p, pl.ds(place, 1), :]
            group, slot = divmod(n, half)
            plane = ref[f % fields, p]
            first = turned(plane, slot)
            last = turned(plane, half + slot + 1 - lanes)
            packed[group] = jnp.where(lane == slot, first, jnp.where(lane == half + slot, last, packed[group]))
    for group, plane in enumerate(packed):
        lanes_ref[group] = plane


def unpack_kernel(above_ref, below_ref, edges_ref):
    fields, depth, rows, lanes = edges_ref.shape
    half = lanes // 2
    lane = lax.broadcasted_iota(jnp.int32, (rows, lanes), 1)
    for f in range(fields):
        for p in range(depth):
            group, slot = divmod(f * depth + p, half)
            above = turned(above_ref[group], -slot)
            below = turned(below_ref[group], lanes - 1 - half - slot)
            edges_ref[f, p] = jnp.where(lane < half, above, below)


def turned(plane, step):
    step = step % plane.shape[1]
    return pltpu.roll(plane, step, 1) if step else plane


def estimate(bytes_accessed):
    return pl.CostEstimate(flops=1_000_000, bytes_accessed=bytes_accessed, transcendentals=0)


def grant():
    return pltpu.CompilerParams(vmem_limit_bytes=16 * 1024 * 1024)


def pack(seed_state, costate):
    fields, depth, rows, lanes = seed_state.shape
    count = 2 * fields * depth
    groups = -(-count // (lanes // 2))
    vmem = pl.BlockSpec(memory_space=pltpu.VMEM)
    shapes = [jax.ShapeDtypeStruct((groups, rows, lanes), jnp.float32)]
    shapes += [jax.ShapeDtypeStruct((count, lanes), jnp.float32)] * (1 if lax.axis_size("gy") == 2 else 2)
    return pl.pallas_call(
        pack_kernel,
        out_shape=shapes,
        in_specs=[vmem] * 2,
        out_specs=[vmem] * len(shapes),
        cost_estimate=estimate(300_000),
        compiler_params=grant(),
    )(seed_state, costate)


def rows_y(packed):
    if len(packed) == 1:
        other = ring(packed[0], "gy", 1)
        return other, other
    first, last = packed
    if lax.axis_size("gy") == 1:
        return first, last
    return line(first, "gy", -1), line(last, "gy", 1)


def lanes_z(packed):
    size = lax.axis_size("gz")
    if size == 1:
        return packed, packed
    if size == 2:
        other = ring(packed, "gz", 1)
        return other, other
    return ring(packed, "gz", -1), ring(packed, "gz", 1)


class Shifts:
    def __init__(self, rows, lanes):
        self.rows, self.lanes = rows, lanes
        self.row = lax.broadcasted_iota(jnp.int32, (rows, lanes), 0)
        self.lane = lax.broadcasted_iota(jnp.int32, (rows, lanes), 1)
        wall, walls = lax.axis_index("gy"), lax.axis_size("gy")
        self.last_wall = jnp.full((rows, lanes), wall, jnp.int32) == walls - 1
        self.first_wall = jnp.full((rows, lanes), wall, jnp.int32) == 0

    def edges(self, above_ref, below_ref, place):
        shape = (self.rows, self.lanes)
        above = jnp.broadcast_to(above_ref[pl.ds(place, 1), :], shape)
        below = jnp.broadcast_to(below_ref[pl.ds(place, 1), :], shape)
        return jnp.where(self.last_wall, 0.0, above), jnp.where(self.first_wall, 0.0, below)

    def y(self, plane, above, below):
        up = jnp.where(self.row == self.rows - 1, above, pltpu.roll(plane, self.rows - 1, 0))
        down = jnp.where(self.row == 0, below, pltpu.roll(plane, 1, 0))
        return up, down

    def z(self, plane, edge):
        up = pltpu.roll(jnp.where(self.lane == 0, edge, plane), self.lanes - 1, 1)
        down = pltpu.roll(jnp.where(self.lane == self.lanes - 1, edge, plane), 1, 1)
        return up, down


def stretch_pull(conf, dual, column):
    out = []
    for m in range(3):
        total = 0.0
        for j in range(3):
            term = dual[COMP[m][j]] * conf[COMP[j][column]]
            total = total + (term + term if j == m else term)
        out.append(total)
    return out


def half_factor(conf):
    return (0.5 * (EXTENSIBILITY - 3.0)) / (EXTENSIBILITY - (conf[0] + conf[1] + conf[2]))


def halo_planes(ref, below, above):
    depth = ref.shape[1]
    return [[below[f]] + [ref[f, p] for p in range(depth)] + [above[f]] for f in range(9)]


def local_kernel(*refs):
    steps_ref, seed_ref, dual_ref, ya_ref, yb_ref, z_ref, raw_ref = refs
    _, depth, rows, lanes = seed_ref.shape
    shift = Shifts(rows, lanes)
    time_step = HORIZON / jnp.full((rows, lanes), steps_ref[0], jnp.int32).astype(jnp.float32)
    nothing = [jnp.zeros((rows, lanes), jnp.float32)] * 9
    seed = halo_planes(seed_ref, nothing, nothing)
    dual = halo_planes(dual_ref, nothing, nothing)
    pull_x = [stretch_pull([c[p] for c in seed[3:]], [c[p] for c in dual[3:]], 0) for p in range(depth + 2)]
    for p in range(depth):
        at = p + 1
        conf = [c[at] for c in seed[3:]]
        pulled = [c[at] for c in dual[3:]]
        seed_y = [shift.edges(ya_ref, yb_ref, f * depth + p) for f in range(9)]
        dual_y = [shift.edges(ya_ref, yb_ref, (9 + f) * depth + p) for f in range(9)]
        seed_z = [z_ref[f, p] for f in range(9)]
        dual_z = [z_ref[9 + f, p] for f in range(9)]
        laps, slopes = [], []
        for f in range(9):
            here = dual[f][at]
            yu, yd = shift.y(here, *dual_y[f])
            zu, zd = shift.z(here, dual_z[f])
            xu, xd = dual[f][at + 1], dual[f][at - 1]
            laps.append((xu + xd) + (yu + yd) + (zu + zd) - 6.0 * here)
            if f < 3:
                slopes.append((0.5 * (xu - xd), 0.5 * (yu - yd), 0.5 * (zu - zd)))
        grads = []
        for f in range(3):
            here = seed[f][at]
            yu, yd = shift.y(here, *seed_y[f])
            zu, zd = shift.z(here, seed_z[f])
            xu, xd = seed[f][at + 1], seed[f][at - 1]
            grads.append((0.5 * (xu - xd), 0.5 * (yu - yd), 0.5 * (zu - zd)))
        pull_y = stretch_pull(conf, pulled, 1)
        pull_z = stretch_pull(conf, pulled, 2)
        above_y = stretch_pull([c[0] for c in seed_y[3:]], [c[0] for c in dual_y[3:]], 1)
        below_y = stretch_pull([c[1] for c in seed_y[3:]], [c[1] for c in dual_y[3:]], 1)
        edge_z = stretch_pull(seed_z[3:], dual_z[3:], 2)
        for m in range(3):
            yu, yd = shift.y(pull_y[m], above_y[m], below_y[m])
            zu, zd = shift.z(pull_z[m], edge_z[m])
            flux = 0.5 * ((pull_x[at + 1][m] - pull_x[at - 1][m]) + (yu - yd) + (zu - zd))
            raw_ref[m, p] = dual[m][at] + time_step * (VISCOSITY * laps[m] - flux)
        half = half_factor(conf)
        stress = []
        for n, (i, j) in enumerate(PAIRS):
            slope = slopes[i][j] if i == j else slopes[i][j] + slopes[j][i]
            stress.append(-(slope + pulled[n]))
        inner = 0.0
        for n in range(6):
            inner = inner + stress[n] * conf[n]
        inner = inner * (half * half) * (2.0 / (EXTENSIBILITY - 3.0))

        def weight(k, j):
            total = 0.0
            for m in range(3):
                term = grads[m][k] * pulled[COMP[m][j]]
                total = total + (term + term if m == j else term)
            return total

        for n, (i, j) in enumerate(PAIRS):
            change = DIFFUSIVITY * laps[3 + n] + half * stress[n]
            change = change + (weight(i, i) + inner if i == j else weight(i, j) + weight(j, i))
            raw_ref[3 + n, p] = pulled[n] + time_step * change


def add_halo(raw, side, time_step, seed_ref, dual_ref, plane, halo_ref):
    half_side = 0.5 * side
    speed = [halo_ref[f] for f in range(3)]
    flow = [halo_ref[9 + f] for f in range(3)]
    dual = [halo_ref[12 + f] for f in range(6)]
    pull = stretch_pull([halo_ref[3 + f] for f in range(6)], dual, 0)
    for m in range(3):
        raw[m] = raw[m] + time_step * (VISCOSITY * flow[m] - half_side * pull[m])
    conf = [seed_ref[3 + f, plane] for f in range(6)]
    pulled = [dual_ref[3 + f, plane] for f in range(6)]
    half = half_factor(conf)
    inner = 0.0
    for j in range(3):
        inner = inner + flow[j] * conf[COMP[0][j]]
    inner = inner * (half * half) * (-half_side * 2.0 / (EXTENSIBILITY - 3.0))
    for n, (i, j) in enumerate(PAIRS):
        change = DIFFUSIVITY * dual[n]
        if i == j:
            change = change + inner
        if i == 0:
            weight = 0.0
            for m in range(3):
                term = speed[m] * pulled[COMP[m][j]]
                weight = weight + (term + term if m == j else term)
            change = change + half_side * (weight - half * flow[j])
        raw[3 + n] = raw[3 + n] + time_step * change


def raw_kernel(start, count, has_below, has_above, *refs):
    steps_ref, seed_ref, dual_ref, local_ref, *halo_refs, raw_ref = refs
    _, depth, rows, lanes = seed_ref.shape
    time_step = HORIZON / jnp.full((rows, lanes), steps_ref[0], jnp.int32).astype(jnp.float32)
    for q in range(count):
        p = start + q
        raw = [local_ref[f, p] for f in range(9)]
        if p == 0 and has_below:
            add_halo(raw, -1.0, time_step, seed_ref, dual_ref, p, halo_refs[0])
        if p == depth - 1 and has_above:
            add_halo(raw, 1.0, time_step, seed_ref, dual_ref, p, halo_refs[-1])
        for f in range(9):
            raw_ref[f, q] = raw[f]


def next_kernel(steps_ref, seed_ref, ya_ref, yb_ref, z_ref, below_ref, above_ref, next_ref):
    _, depth, rows, lanes = seed_ref.shape
    shift = Shifts(rows, lanes)
    time_step = HORIZON / jnp.full((rows, lanes), steps_ref[0], jnp.int32).astype(jnp.float32)
    seed = halo_planes(seed_ref, [below_ref[f] for f in range(9)], [above_ref[f] for f in range(9)])
    halves = [half_factor([c[p] for c in seed[3:]]) for p in range(depth + 2)]
    for p in range(depth):
        at = p + 1
        conf = [c[at] for c in seed[3:]]
        ey = [shift.edges(ya_ref, yb_ref, f * depth + p) for f in range(9)]
        ez = [z_ref[f, p] for f in range(9)]
        laps, grads = [], []
        for f in range(9):
            here = seed[f][at]
            yu, yd = shift.y(here, *ey[f])
            zu, zd = shift.z(here, ez[f])
            xu, xd = seed[f][at + 1], seed[f][at - 1]
            laps.append((xu + xd) + (yu + yd) + (zu + zd) - 6.0 * here)
            if f < 3:
                grads.append((0.5 * (xu - xd), 0.5 * (yu - yd), 0.5 * (zu - zd)))
        half = halves[at]
        half_above, half_below = half_factor([c[0] for c in ey[3:]]), half_factor([c[1] for c in ey[3:]])
        half_z = half_factor(ez[3:])
        for i in range(3):
            cx, cy, cz = COMP[i]
            yu, yd = shift.y(half * conf[cy], half_above * ey[3 + cy][0], half_below * ey[3 + cy][1])
            zu, zd = shift.z(half * conf[cz], half_z * ez[3 + cz])
            xu = halves[at + 1] * seed[3 + cx][at + 1]
            xd = halves[at - 1] * seed[3 + cx][at - 1]
            divergence = 0.5 * ((xu - xd) + (yu - yd) + (zu - zd))
            next_ref[i, p] = seed[i][at] + time_step * (VISCOSITY * laps[i] + divergence)
        for n, (i, j) in enumerate(PAIRS):
            stretch = 0.0
            for k in range(3):
                term = grads[i][k] * conf[COMP[k][j]]
                stretch = stretch + (term + term if i == j else term + grads[j][k] * conf[COMP[k][i]])
            stress = half * conf[n] - (0.5 if i == j else 0.0)
            next_ref[3 + n, p] = conf[n] + time_step * (DIFFUSIVITY * laps[3 + n] + stretch - stress)


def average_kernel(planes, *refs):
    raw_ref, image_ref, *_, out_ref, mean_ref, sem = refs
    for f, sign in enumerate(SIGNS):
        for q in range(raw_ref.shape[1]):
            raw, image = raw_ref[f, q], image_ref[f, q]
            mean_ref[f, q] = 0.5 * (raw + image if sign > 0 else raw - image)
    copy = pltpu.make_async_copy(mean_ref, out_ref.at[:, planes], sem)
    copy.start()
    copy.wait()


def average(start, shape, raw, image, so_far):
    vmem = pl.BlockSpec(memory_space=pltpu.VMEM)
    hbm = pl.BlockSpec(memory_space=pltpu.HBM)
    earlier = () if so_far is None else (so_far,)
    return pl.pallas_call(
        functools.partial(average_kernel, pl.ds(start, raw.shape[1])),
        out_shape=jax.ShapeDtypeStruct(shape, jnp.float32),
        in_specs=[vmem] * 2 + [hbm] * len(earlier),
        out_specs=hbm,
        scratch_shapes=[pltpu.VMEM(raw.shape, jnp.float32), pltpu.SemaphoreType.DMA],
        input_output_aliases={2: 0} if earlier else {},
        cost_estimate=estimate(1_000_000),
        compiler_params=grant(),
    )(raw, image, *earlier)


def call(kernel, shape, steps, *arrays):
    vmem = pl.BlockSpec(memory_space=pltpu.VMEM)
    scalars = [pl.BlockSpec(memory_space=pltpu.SMEM)] * len(steps)
    return pl.pallas_call(
        kernel,
        out_shape=jax.ShapeDtypeStruct(shape, jnp.float32),
        in_specs=scalars + [vmem] * len(arrays),
        out_specs=vmem,
        cost_estimate=estimate(1_000_000),
        compiler_params=grant(),
    )(*steps, *arrays)


def per_device(seed_state, costate, step_count):
    depth = seed_state.shape[1]
    first, last = faces(seed_state, costate)
    below = ring(last, "gx", 1)
    above = ring(first, "gx", -1)
    lanes, *rows = pack(seed_state, costate)
    ya, yb = rows_y(rows)
    z = call(unpack_kernel, (18,) + seed_state.shape[1:], (), *lanes_z(lanes))
    local = call(local_kernel, seed_state.shape, (step_count,), seed_state, costate, ya, yb, z)
    walls = lax.axis_size("gy")
    gradient = None
    for start, count in ((0, depth - 1), (depth - 1, 1)):
        if count == 0:
            continue
        has_below, has_above = start == 0, start + count == depth
        raw = call(
            functools.partial(raw_kernel, start, count, has_below, has_above),
            (9, count) + seed_state.shape[2:],
            (step_count,),
            *(seed_state, costate, local),
            *((below,) if has_below else ()),
            *((above,) if has_above else ()),
        )
        partner = lax.ppermute(raw, "gy", [(i, walls - 1 - i) for i in range(walls)])
        gradient = average(start, seed_state.shape, raw, jnp.flip(partner, axis=2), gradient)
    next_state = call(next_kernel, seed_state.shape, (step_count,), seed_state, ya, yb, z, below, above)
    return next_state, gradient


def solution(mesh):
    placed = P(None, ("rep", "gx"), "gy", "gz")
    return jax.shard_map(
        per_device,
        mesh=mesh,
        in_specs=(placed, placed, P("rep")),
        out_specs=(placed, placed),
        check_vma=False,
    )
```
